512 devices in a mesh: patch: 32 (over z, core), line: 16 (over x, y).
Axes of the slice: x: 4, y: 4, z: 16, core: 2. Of those that a mesh axis runs over, the one named last changes fastest.
Arguments:
- residual: float32 [128, 32, 100], P('patch', 'line'), may hold values from -2 to 2
- previous_adjoint: float32 [128, 32, 100], P('patch', 'line'), may hold values from -6 to 6
- lower_factor: float32 [128, 32, 100, 100], P('patch', 'line'), may hold values from -0.625 to 0.625
- pivot_inverse: float32 [128, 32, 100, 100], P('patch', 'line'), may hold values from -0.3 to 1.7, as said below
- upper_factor: float32 [128, 32, 100, 100], P('patch', 'line'), may hold values from -0.5 to 0.5
- face_couple: float32 [128, 32, 4, 100, 50], P('patch', 'line'), may hold values from -0.21875 to 0.21875
- face_restrict: float32 [4, 50, 100], replicated, may hold values from -0.625 to 0.625
- neighbours: int32 [128, 4], P('patch'), may hold values from 0 to 47
Outputs:
- adjoint: float32 [128, 32, 100], P('patch', 'line')
The draws below stay inside these ranges and needn't reach their ends.
Inputs may be any that keep to these rules, and one draw needn't show every extreme that they name: `pivot_inverse`: each block is a diagonal between 0.6 and 1.4 plus a full part whose entries lie within 0.3 of zero.
All inputs are finite; a program needn't handle non-finite values.
Results may differ from the reference program's by a relative error of at most 0.00028.
Values sent between devices are 32-bit elements; how exact they have to be, the bound alone decides.
A program may use at most 64 MiB of HBM per device.

```python
import jax
import jax.numpy as jnp
from jax import lax

B = 100
F = 50
NFACE = 4
SWEEPS = 2
LPD = 4
LINES = 128
LEN = 32
N_PATCH = 32


def draw_pivot_inverse(key, part):
    key_diag, key_off = jax.random.split(key)
    diagonal = jax.random.uniform(key_diag, (LINES, LEN, B), jnp.float32, 0.6, 1.4)
    offdiag = jax.random.normal(key_off, (LINES, LEN, B, B), jnp.float32) * (0.3 / jnp.sqrt(jnp.float32(B)))
    offdiag = jnp.clip(offdiag, -0.3, 0.3)
    rows = lax_rows(B)
    return offdiag + rows * diagonal[..., None]


def lax_rows(width):
    first = jnp.arange(width, dtype=jnp.int32)[:, None]
    second = jnp.arange(width, dtype=jnp.int32)[None, :]
    return (first == second).astype(jnp.float32)


def set_ends(array, key, least, largest):
    index_at = [jax.random.randint(jax.random.fold_in(key, axis), (), 0, length) for axis, length in enumerate(array.shape)]
    main_axis = array.shape.index(max(array.shape))
    beside = index_at[:main_axis] + [(index_at[main_axis] + 1) % array.shape[main_axis]] + index_at[main_axis + 1:]
    return array.at[tuple(index_at)].set(least).at[tuple(beside)].set(largest)


def shard_levels(rng, extent, cuts, smallest, high):
    def one(position, shards_of):
        heights = jax.random.uniform(jax.random.fold_in(jax.random.fold_in(rng, 6), position), (shards_of,), jnp.float32, smallest / len(cuts), high / len(cuts))
        return jnp.repeat(jnp.exp(heights), extent[position] // shards_of).reshape((-1,) + (1,) * (len(extent) - position - 1))

    gain = one(*cuts[0])
    for cut in cuts[1:]:
        gain = gain * one(*cut)
    return gain


def noise(stream_key, extent, scale, reach, cuts=(), kind=jnp.bfloat16):
    values = jax.random.normal(stream_key, extent, jnp.float32) * scale
    if len(cuts) > 0:
        values = shard_levels(stream_key, extent, cuts, -0.22, 0.18) * values
    return jnp.clip(values, min=-reach, max=reach).astype(kind)


def setup_inputs(seed: int = 0) -> dict:
    seeds = jax.random.split(jax.random.key(seed), 9)
    residual = noise(seeds[0], (LINES, LEN, B), 0.3, 2.0, ((0, 32), (1, 16)), jnp.float32)
    previous_adjoint = noise(seeds[1], (LINES, LEN, B), 1.0, 6.0, ((0, 32), (1, 16)), jnp.float32)
    lower_factor = noise(seeds[2], (LINES, LEN, B, B), (B + B // 16) ** -0.5, 0.625, ((0, 32), (1, 16)), jnp.float32)
    pivot_inverse = draw_pivot_inverse(jax.random.fold_in(seeds[8], 71), 0)
    upper_factor = noise(seeds[4], (LINES, LEN, B, B), (B + 2 * B // 5) ** -0.5, 0.5, ((0, 32), (1, 16)), jnp.float32)
    face_couple = noise(seeds[5], (LINES, LEN, NFACE, B, F), (4 * NFACE * F) ** -0.5, 0.21875, ((0, 32), (1, 16)), jnp.float32)
    face_restrict = noise(seeds[6], (NFACE, F, B), B ** -0.5, 0.625, (), jnp.float32)
    neighbours = set_ends(jax.random.randint(seeds[7], (LINES, NFACE), 0, 3 * LPD * NFACE), jax.random.fold_in(seeds[7], 1), 0, (3 * LPD * NFACE) - 1).astype(jnp.int32)
    return dict(residual=residual, previous_adjoint=previous_adjoint, lower_factor=lower_factor, pivot_inverse=pivot_inverse, upper_factor=upper_factor, face_couple=face_couple, face_restrict=face_restrict, neighbours=neighbours)


HIGH = lax.Precision.HIGHEST


def coupling(field, face_restrict, face_couple, neighbours):
    traces = jnp.einsum("fkb,nlb->nflk", face_restrict, field, precision=HIGH)
    per_patch = LPD * NFACE
    offset = neighbours // per_patch - 1
    remain = neighbours % per_patch
    patch_of = (jnp.arange(field.shape[0], dtype=jnp.int32) // LPD)[:, None]
    source_line = (((patch_of + offset) % N_PATCH) * LPD + remain // NFACE).astype(jnp.int32)
    source_face = (remain % NFACE).astype(jnp.int32)
    picked = traces[source_line, source_face]
    return jnp.einsum("nlfbk,nflk->nlb", face_couple, picked, precision=HIGH)


def line_solve(rhs, lower_factor, pivot_inverse, upper_factor):
    start = jnp.zeros((rhs.shape[0], rhs.shape[2]), jnp.float32)

    def forward(carry, item):
        block, value = item
        result = value - jnp.einsum("nab,nb->na", block, carry, precision=HIGH)
        return result, result

    _, ys = lax.scan(forward, start, (jnp.moveaxis(lower_factor, 1, 0), jnp.moveaxis(rhs, 1, 0)))

    def backward(carry, item):
        pivot, upper, value = item
        inner = value - jnp.einsum("nab,nb->na", upper, carry, precision=HIGH)
        result = jnp.einsum("nab,nb->na", pivot, inner, precision=HIGH)
        return result, result

    _, xs = lax.scan(backward, start, (jnp.moveaxis(pivot_inverse, 1, 0), jnp.moveaxis(upper_factor, 1, 0), ys), reverse=True)
    return jnp.moveaxis(xs, 0, 1)


def reference(residual, previous_adjoint, lower_factor, pivot_inverse, upper_factor, face_couple, face_restrict, neighbours):
    field = previous_adjoint
    for sweep in range(SWEEPS):
        rhs = residual - coupling(field, face_restrict, face_couple, neighbours)
        field = line_solve(rhs, lower_factor, pivot_inverse, upper_factor)
    return field
```

```python
import jax
import jax.numpy as jnp
from jax import lax
from jax.experimental import pallas as pl
from jax.experimental.pallas import tpu as pltpu
from jax.sharding import PartitionSpec as P

F32 = jnp.float32
BF16 = jnp.bfloat16
MESH = pl.DeviceIdType.MESH
B = 100
Q = 200
NP = 32
NN = (((1,), (0,)), ((), ()))
NT = (((1,), (1,)), ((), ()))


def split(a):
    high = a.astype(BF16)
    return high, (a - high.astype(F32)).astype(BF16)


def dot3(a, b, dims):
    ah, al = split(a)
    bh, bl = split(b)

    def mm(u, v):
        return lax.dot_general(u, v, dims, preferred_element_type=F32)

    return mm(ah, bh) + (mm(ah, bl) + mm(al, bh))


def kernel(
    nb, res, prev, low, piv, upp, fc, rst, out,
    rl, rd, ru, rf, fown, hb, rhs_out, rhs_in, eb, zxb, zs, hb2, th, fx, f8, lhs, ob,
    s_loc, s_raw, r_raw, s_h0, r_h0, s_a, r_a, s_x, r_x, s_h1, r_h1, s_t, r_t, s_o, r_o,
):
    p = lax.axis_index("patch")
    line = lax.axis_index("line")
    x, y = line // 4, line % 4

    def y_peer(d):
        return (p, x * 4 + (y + d) % 4)

    def x_peer(d):
        return (p, ((x + d) % 4) * 4 + y)

    def remote(src, dst, send, recv, device):
        return pltpu.make_async_remote_copy(
            src_ref=src, dst_ref=dst, send_sem=send, recv_sem=recv,
            device_id=device, device_id_type=MESH,
        )

    raws = ((low, rl), (piv, rd), (upp, ru), (fc, rf))
    local = [pltpu.make_async_copy(fc, fown, s_loc.at[4])]
    for k, (src, dst) in enumerate(raws):
        local.append(pltpu.make_async_copy(src.at[y], dst.at[y], s_loc.at[k]))
    for copy in local:
        copy.start()

    around = [
        (dp, dy) for dp in (-1, 0, 1) for dy in range(4) if (dp, dy) != (0, 0)
    ]

    def around_peer(dp, dy):
        return ((p + dp + NP) % NP, x * 4 + (y + dy) % 4)

    barrier = pltpu.get_barrier_semaphore()
    for dp, dy in around:
        pl.semaphore_signal(
            barrier, inc=1, device_id=around_peer(dp, dy), device_id_type=MESH
        )
    for d in (1, 2, 3):
        pl.semaphore_signal(barrier, inc=1, device_id=x_peer(d), device_id_type=MESH)

    halo = dot3(prev[...], rst[...], NT)
    for n in range(4):
        hb[4 + n, :, :Q] = halo[2 * n : 2 * n + 2]
    pl.semaphore_wait(barrier, 14)

    sends = []
    halos = []
    for i, dp in enumerate((1, -1)):
        copy = remote(
            hb.at[pl.ds(4, 4)], hb.at[pl.ds((1 - dp) * 4, 4)], s_h0.at[i], r_h0.at[i],
            ((p + dp + NP) % NP, line),
        )
        copy.start()
        halos.append(copy)
    sends += halos
    raw = {}
    for k, (src, dst) in enumerate(raws):
        for d in (1, 3, 2):
            copy = remote(
                src.at[(y + d) % 4], dst.at[y], s_raw.at[k, d - 1], r_raw.at[k, d - 1],
                y_peer(d),
            )
            copy.start()
            raw[k, d] = copy
            sends.append(copy)

    lane = lax.broadcasted_iota(jnp.int32, (8, Q), 1) % 4

    def pick(block, source, f):
        total = jnp.zeros(block.shape, F32)
        for g in range(4):
            moved = block if g == f else pltpu.roll(block, (f - g) % 256, axis=1)
            total = jnp.where(source == g, moved, total)
        return jnp.where(lane[: block.shape[0]] == f, total[:, :Q], 0.0)

    for copy in halos:
        copy.wait_recv()
    for n in range(4):
        picked = jnp.zeros((2, Q), F32)
        for f in range(4):
            entry = nb[n, f]
            picked = picked + pick(hb[entry // 4], entry % 4, f)
        lhs[2 * n : 2 * n + 2, :Q] = picked
    local[0].wait()
    whole = lhs[:, :Q]
    for n in range(4):
        for e in range(2):
            row = 2 * n + e
            got = dot3(whole, fown[n, e], NN)
            rhs_out[n, e : e + 1, :B] = res[row : row + 1, :] - got[row : row + 1, :]
        rhs_out[n, 2:4, :B] = res[2 * n : 2 * n + 2, :]
    rhs_in[y] = rhs_out[y]
    there = []
    for d in (1, 3, 2):
        copy = remote(
            rhs_out.at[(y + d) % 4], rhs_in.at[y], s_a.at[d - 1], r_a.at[d - 1], y_peer(d)
        )
        copy.start()
        there.append(copy)
    sends += there

    for copy in local[1:4]:
        copy.wait()
    for k in range(3):
        for d in (1, 3, 2):
            raw[k, d].wait_recv()

    def block(ref, l):
        return ref[l // 2, pl.ds(l % 2, B, stride=2), :]

    for l in range(8):
        eb[l, :B, :B] = dot3(block(rd, l), block(ru, l), NN)
    for copy in there:
        copy.wait_recv()

    rows = lax.broadcasted_iota(jnp.int32, (104, B), 0)
    columns = lax.broadcasted_iota(jnp.int32, (104, B), 1)
    unit = jnp.where(rows == columns, 1.0, 0.0).astype(F32)
    eye = rows[:B] == columns[:B]

    def rhs_row(l):
        return rhs_in[l // 2, l % 2 : l % 2 + 1, :B]

    zy = unit
    for l in range(8):
        zy = jnp.where(rows == B, rhs_row(l), 0.0) - dot3(zy, block(rl, l), NT)
        zxb[l, :104, :B] = dot3(zy, block(rd, l), NT)
    zs[x, :104, :B] = zy
    after = jnp.concatenate([jnp.zeros((104, B), F32), unit], axis=0)
    for l in range(7, -1, -1):
        moved = dot3(after, eb[l, :B, :B], NT)
        after = jnp.concatenate([zxb[l, :104, :B] - moved[:104], -moved[104:]], axis=0)
        zxb[l, :, :B] = after
    zs[x, 104:, :B] = after
    there = []
    for d in (1, 3, 2):
        copy = remote(zs.at[x], zs.at[x], s_x.at[d - 1], r_x.at[d - 1], x_peer(d))
        copy.start()
        there.append(copy)
    sends += there

    def column(row):
        return jnp.sum(jnp.where(eye, row, 0.0), axis=1, keepdims=True)

    def times(row, matrix):
        return jnp.sum(matrix * column(row), axis=0, keepdims=True)

    def apply(matrix, row):
        got = jnp.sum(matrix * row, axis=1, keepdims=True)
        return jnp.sum(jnp.where(eye, got, 0.0), axis=0, keepdims=True)

    def entries(tail, head):
        y2 = tail[1] + times(tail[0], zs[1, :B, :B])
        y3 = tail[2] + times(y2, zs[2, :B, :B])
        h3 = head[3] + times(y3, zs[3, 104:204, :B])
        h2 = head[2] + times(y2, zs[2, 104:204, :B]) + times(h3, zs[2, 208:308, :B])
        h1 = head[1] + times(tail[0], zs[1, 104:204, :B]) + times(h2, zs[1, 208:308, :B])
        zero = jnp.zeros((1, B), F32)

        def mine(values):
            total = values[0]
            for at in range(1, 4):
                total = jnp.where(x == at, values[at], total)
            return total

        return mine((zero, tail[0], y2, y3)), mine((h1, h2, h3, zero))

    def corrected(base, y_in, x_in):
        y_col, x_col = column(y_in), column(x_in)
        values = []
        for l in range(8):
            more = zxb[l, :B, :B] * y_col + zxb[l, 104:204, :B] * x_col
            values.append(base[l] + jnp.sum(more, axis=0, keepdims=True))
        return values

    for copy in there:
        copy.wait_recv()
    y_in, x_in = entries(
        [zs[at, B : B + 1, :B] for at in range(4)],
        [zs[at, 204:205, :B] for at in range(4)],
    )
    field = corrected([zxb[l, B : B + 1, :B] for l in range(8)], y_in, x_in)
    for l in range(8):
        f8[l : l + 1, :B] = field[l]

    hb2[4 + y, :, :Q] = dot3(f8[:, :B], rst[...], NT)
    there = []
    for i, (dp, dy) in enumerate(around):
        copy = remote(
            hb2.at[4 + y], hb2.at[(1 - dp) * 4 + y], s_h1.at[i], r_h1.at[i], around_peer(dp, dy)
        )
        copy.start()
        there.append(copy)
    sends += there
    local[4].wait()
    for d in (1, 3, 2):
        raw[3, d].wait_recv()
    for copy in there:
        copy.wait_recv()
    picked = jnp.zeros((8, Q), F32)
    for f in range(4):
        entry = nb[y, f]
        picked = picked + pick(hb2[entry // 4], entry % 4, f)
    ys = []
    for l in range(8):
        got = dot3(picked, rf[l // 2, l % 2], NN)
        value = res_owner(l, rhs_in) - got[l : l + 1, :]
        if l:
            value = value - apply(block(rl, l), ys[-1])
        ys.append(value)
    base = [None] * 8
    for l in range(7, -1, -1):
        base[l] = apply(block(rd, l), ys[l])
        if l < 7:
            base[l] = base[l] - apply(eb[l, :B, :B], base[l + 1])
    th[x, 0:1, :B] = ys[7]
    th[x, 1:2, :B] = base[0]
    there = []
    for d in (1, 3, 2):
        copy = remote(th.at[x], th.at[x], s_t.at[d - 1], r_t.at[d - 1], x_peer(d))
        copy.start()
        there.append(copy)
    sends += there
    for copy in there:
        copy.wait_recv()
    y_in, x_in = entries(
        [th[at, 0:1, :B] for at in range(4)], [th[at, 1:2, :B] for at in range(4)]
    )
    field = corrected(base, y_in, x_in)
    for l in range(8):
        fx[l // 2, l % 2 : l % 2 + 1, :B] = field[l]
    ob[y] = fx[y]
    there = []
    for d in (1, 3, 2):
        copy = remote(fx.at[(y + d) % 4], ob.at[y], s_o.at[d - 1], r_o.at[d - 1], y_peer(d))
        copy.start()
        there.append(copy)
    sends += there
    for copy in there:
        copy.wait_recv()
    for n in range(4):
        out[2 * n : 2 * n + 2, :] = ob[n, :, :B]
    for copy in sends:
        copy.wait_send()


def res_owner(l, ref):
    return ref[l // 2, 2 + l % 2 : 3 + l % 2, :B]


def per_device(residual, previous, lower, pivot, upper, couple, restrict, neighbours):
    def factor(a):
        return jnp.transpose(a, (0, 2, 1, 3)).reshape(4, 2 * B, B)

    vmem = pl.BlockSpec(memory_space=pltpu.VMEM)
    anywhere = pl.BlockSpec(memory_space=pl.ANY)
    dma = pltpu.SemaphoreType.DMA
    result = pl.pallas_call(
        kernel,
        out_shape=jax.ShapeDtypeStruct((8, B), F32),
        in_specs=[pl.BlockSpec(memory_space=pltpu.SMEM), vmem, vmem]
        + [anywhere] * 4
        + [vmem],
        out_specs=vmem,
        scratch_shapes=[
            pltpu.VMEM((4, 2 * B, B), F32),
            pltpu.VMEM((4, 2 * B, B), F32),
            pltpu.VMEM((4, 2 * B, B), F32),
            pltpu.VMEM((4, 2, Q, B), F32),
            pltpu.VMEM((4, 2, Q, B), F32),
            pltpu.VMEM((12, 2, 256), F32),
            pltpu.VMEM((4, 4, 128), F32),
            pltpu.VMEM((4, 4, 128), F32),
            pltpu.VMEM((8, 104, 128), F32),
            pltpu.VMEM((8, 208, 128), F32),
            pltpu.VMEM((4, 312, 128), F32),
            pltpu.VMEM((12, 8, 256), F32),
            pltpu.VMEM((4, 8, 128), F32),
            pltpu.VMEM((4, 2, 128), F32),
            pltpu.VMEM((8, 128), F32),
            pltpu.VMEM((8, 256), F32),
            pltpu.VMEM((4, 2, 128), F32),
            dma((5,)),
            dma((4, 3)),
            dma((4, 3)),
            dma((2,)),
            dma((2,)),
            dma((3,)),
            dma((3,)),
            dma((3,)),
            dma((3,)),
            dma((11,)),
            dma((11,)),
            dma((3,)),
            dma((3,)),
            dma((3,)),
            dma((3,)),
        ],
        compiler_params=pltpu.CompilerParams(
            collective_id=0, has_side_effects=True, vmem_limit_bytes=40 << 20
        ),
    )(
        neighbours,
        residual.reshape(8, B),
        previous.reshape(8, B),
        factor(lower),
        factor(pivot),
        factor(upper),
        jnp.transpose(couple, (0, 1, 4, 2, 3)).reshape(4, 2, Q, B),
        jnp.transpose(restrict, (1, 0, 2)).reshape(Q, B),
    )
    return result.reshape(4, 2, B)


def solution(mesh):
    placed = (
        P("patch", "line", None),
        P("patch", "line", None),
        P("patch", "line", None, None),
        P("patch", "line", None, None),
        P("patch", "line", None, None),
        P("patch", "line", None, None, None),
        P(),
        P("patch", None),
    )
    return jax.shard_map(
        per_device, mesh=mesh, in_specs=placed, out_specs=P("patch", "line", None), check_vma=False
    )
```

```python
import jax
import jax.numpy as jnp
from jax import lax
from jax.experimental import pallas as pl
from jax.experimental.pallas import tpu as pltpu
from jax.sharding import PartitionSpec as P

F32 = jnp.float32
BF16 = jnp.bfloat16
MESH = pl.DeviceIdType.MESH
B = 100
Q = 200
NP = 32
NN = (((1,), (0,)), ((), ()))
NT = (((1,), (1,)), ((), ()))
ORDER = (1, 3, 2)


def split(a):
    high = a.astype(BF16)
    return high, (a - high.astype(F32)).astype(BF16)


def dot3(a, b, dims=NN):
    ah, al = split(a)
    bh, bl = split(b)

    def mm(u, v):
        return lax.dot_general(u, v, dims, preferred_element_type=F32)

    return mm(ah, bh) + (mm(ah, bl) + mm(al, bh))


def kernel(
    nb_any, res_any, prev_any, rst_any, low, piv, upp, fc, out,
    nb, res, prev, rst, lo, di, up, fo,
    eb, wb, seg_out, seg_in, quarter, part, hb_first, hb_second, lhs, f8,
    a_out, a_in, th, en_out, en_in,
    s_loc, s_m, r_m, s_q, r_q, s_h, r_h, s_a, r_a, s_x, r_x, s_e, r_e,
):
    p = lax.axis_index("patch")
    line = lax.axis_index("line")
    x, y = line // 4, line % 4

    def y_peer(d):
        return (p, x * 4 + (y + d) % 4)

    def x_peer(d):
        return (p, ((x + d) % 4) * 4 + y)

    def z_peer(d):
        return ((p + d + NP) % NP, line)

    def remote(src, dst, send, recv, device):
        return pltpu.make_async_remote_copy(
            src_ref=src, dst_ref=dst, send_sem=send, recv_sem=recv,
            device_id=device, device_id_type=MESH,
        )

    barrier = pltpu.get_barrier_semaphore()
    for d in (1, 2, 3):
        pl.semaphore_signal(barrier, inc=1, device_id=y_peer(d), device_id_type=MESH)
        pl.semaphore_signal(barrier, inc=1, device_id=x_peer(d), device_id_type=MESH)
    for d in (1, -1):
        pl.semaphore_signal(barrier, inc=1, device_id=z_peer(d), device_id_type=MESH)
    pairs = (
        (low, lo), (prev_any, prev), (rst_any, rst), (piv, di), (upp, up),
        (nb_any, nb), (res_any, res), (fc, fo),
    )
    local = [
        pltpu.make_async_copy(src, dst, s_loc.at[k]) for k, (src, dst) in enumerate(pairs)
    ]
    for copy in local:
        copy.start()

    hb = (hb_first, hb_second)
    sends = []
    eye = lax.broadcasted_iota(jnp.int32, (B, B), 0) == lax.broadcasted_iota(
        jnp.int32, (B, B), 1
    )

    def to_row(column):
        return jnp.sum(jnp.where(eye, column, 0.0), axis=0, keepdims=True)

    def apply(matrix, row):
        return to_row(jnp.sum(matrix * row, axis=1, keepdims=True))

    def apply2(one, u, two, v):
        return to_row(jnp.sum(one * u + two * v, axis=1, keepdims=True))

    def element(ref, n, l):
        return ref[n, pl.ds(l, B, stride=2), :]

    def seg(k, j):
        return seg_in[k, j, :B, :B]

    def own(k, n):
        return seg_out[k, n, :B, :B]

    def send_halo(sweep, field):
        halo = dot3(field, rst[...], NT)
        for n in range(4):
            hb[sweep][4 + n, :, :Q] = halo[2 * n : 2 * n + 2]
        if sweep == 0:
            pl.semaphore_wait(barrier, 8)
        copies = []
        for i, dp in enumerate((1, -1)):
            copy = remote(
                hb[sweep].at[pl.ds(4, 4)], hb[sweep].at[pl.ds((1 - dp) * 4, 4)],
                s_h.at[sweep, i], r_h.at[sweep, i], z_peer(dp),
            )
            copy.start()
            copies.append(copy)
        sends.extend(copies)
        return copies

    def send_maps(k):
        copies = []
        for d in ORDER:
            copy = remote(
                seg_out.at[k, (y + d) % 4], seg_in.at[k, y],
                s_m.at[k, d - 1], r_m.at[k, d - 1], y_peer(d),
            )
            copy.start()
            copies.append(copy)
        sends.extend(copies)
        seg_in[k, y] = seg_out[k, y]
        return copies

    def send_quarter(k, value):
        quarter[x, k, :B, :B] = value
        copies = []
        for d in ORDER:
            copy = remote(
                quarter.at[x, k], quarter.at[x, k], s_q.at[k, d - 1], r_q.at[k, d - 1], x_peer(d)
            )
            copy.start()
            copies.append(copy)
        sends.extend(copies)
        return copies

    lane = lax.broadcasted_iota(jnp.int32, (2, Q), 1) % 4

    def pick(block, source, f):
        total = jnp.zeros(block.shape, F32)
        for g in range(4):
            moved = block if g == f else pltpu.roll(block, (f - g) % 256, axis=1)
            total = jnp.where(source == g, moved, total)
        return jnp.where(lane == f, total[:, :Q], 0.0)

    def right_sides(sweep):
        for n in range(4):
            picked = jnp.zeros((2, Q), F32)
            for f in range(4):
                entry = nb[n, f]
                picked = picked + pick(hb[sweep][entry // 4], entry % 4, f)
            lhs[2 * n : 2 * n + 2, :] = picked
        whole = lhs[...]
        rows = []
        for row in range(8):
            got = dot3(whole, fo[row // 2, row % 2])
            rows.append(res[row : row + 1, :] - got[row : row + 1, :])
        return rows

    def send_local(sweep, rows):
        tails, heads = [], []
        for n in range(4):
            tails.append(rows[2 * n + 1] - apply(element(lo, n, 1), rows[2 * n]))
        for n in range(4):
            heads.append(apply2(element(di, n, 0), rows[2 * n], wb[n, :B, :B], -tails[n]))
            a_out[sweep, n, 0:1, :B] = tails[n]
            a_out[sweep, n, 1:2, :B] = heads[n]
        copies = []
        for d in ORDER:
            copy = remote(
                a_out.at[sweep, (y + d) % 4], a_in.at[sweep, y],
                s_a.at[sweep, d - 1], r_a.at[sweep, d - 1], y_peer(d),
            )
            copy.start()
            copies.append(copy)
        sends.extend(copies)
        a_in[sweep, y] = a_out[sweep, y]
        return copies, tails, heads

    def quarter_tail(sweep):
        tail = [a_in[sweep, j, 0:1, :B] for j in range(4)]
        y2 = tail[1] + apply(seg(0, 1), tail[0])
        y3 = tail[2] + apply(seg(0, 2), y2)
        return (None, tail[0], y2, y3), tail[3] + apply(seg(0, 3), y3)

    def send_quarter_vectors(sweep, starts, tail):
        head = [a_in[sweep, j, 1:2, :B] for j in range(4)]
        g3 = head[3] + apply(seg(2, 3), starts[3])
        g2 = head[2] + apply2(seg(2, 2), starts[2], seg(1, 2), g3)
        g1 = head[1] + apply2(seg(2, 1), starts[1], seg(1, 1), g2)
        th[sweep, x, 0:1, :B] = tail
        th[sweep, x, 1:2, :B] = head[0] + apply(seg(1, 0), g1)
        copies = []
        for d in ORDER:
            copy = remote(
                th.at[sweep, x], th.at[sweep, x], s_x.at[sweep, d - 1], r_x.at[sweep, d - 1], x_peer(d)
            )
            copy.start()
            copies.append(copy)
        sends.extend(copies)
        return copies, (g1, g2, g3)

    def mine(values):
        total = values[0]
        for at in range(1, 4):
            total = jnp.where(x == at, values[at], total)
        return total

    def send_entries(sweep, starts, ends):
        def q(at, k):
            return quarter[at, k, :B, :B]

        tail = [th[sweep, at, 0:1, :B] for at in range(4)]
        head = [th[sweep, at, 1:2, :B] for at in range(4)]
        zero = jnp.zeros((1, B), F32)
        y2 = tail[1] + apply(q(1, 0), tail[0])
        y3 = tail[2] + apply(q(2, 0), y2)
        h3 = head[3] + apply(q(3, 2), y3)
        h2 = head[2] + apply2(q(2, 2), y2, q(2, 1), h3)
        h1 = head[1] + apply2(q(1, 2), tail[0], q(1, 1), h2)
        y_in = mine((zero, tail[0], y2, y3))
        x_in = mine((h1, h2, h3, zero))
        en_out[sweep, 0, 0:1, :B] = y_in
        en_out[sweep, 1, 0:1, :B] = starts[1] + apply(seg(0, 0), y_in)
        en_out[sweep, 2, 0:1, :B] = starts[2] + apply(part[0, :B, :B], y_in)
        en_out[sweep, 3, 0:1, :B] = starts[3] + apply(part[1, :B, :B], y_in)
        en_out[sweep, 0, 1:2, :B] = ends[0] + apply2(
            part[4, :B, :B], y_in, part[6, :B, :B], x_in
        )
        en_out[sweep, 1, 1:2, :B] = ends[1] + apply2(
            part[3, :B, :B], y_in, part[5, :B, :B], x_in
        )
        en_out[sweep, 2, 1:2, :B] = ends[2] + apply2(part[2, :B, :B], y_in, seg(1, 3), x_in)
        en_out[sweep, 3, 1:2, :B] = x_in
        copies = []
        for d in ORDER:
            copy = remote(
                en_out.at[sweep, (y + d) % 4], en_in.at[sweep, y],
                s_e.at[sweep, d - 1], r_e.at[sweep, d - 1], y_peer(d),
            )
            copy.start()
            copies.append(copy)
        sends.extend(copies)
        en_in[sweep, y] = en_out[sweep, y]
        return copies

    def arrived(copies):
        for copy in copies:
            copy.wait_recv()

    def fields(sweep, tails, heads, store):
        for n in range(4):
            y_in = en_in[sweep, n, 0:1, :B]
            x_in = en_in[sweep, n, 1:2, :B]
            tail = tails[n] + apply(own(0, n), y_in)
            store(2 * n, heads[n] + apply2(own(2, n), y_in, own(1, n), x_in))
            store(2 * n + 1, apply2(element(di, n, 1), tail, eb[1, n, :B, :B], -x_in))

    local[0].wait()
    for n in range(4):
        seg_out[0, n, :B, :B] = dot3(element(lo, n, 1), element(lo, n, 0))
    local[1].wait()
    local[2].wait()
    halos = send_halo(0, prev[...])
    maps0 = send_maps(0)
    local[3].wait()
    local[4].wait()
    for n in range(4):
        for l in range(2):
            eb[l, n, :B, :B] = dot3(element(di, n, l), element(up, n, l))
        seg_out[1, n, :B, :B] = dot3(eb[0, n, :B, :B], eb[1, n, :B, :B])
    maps1 = send_maps(1)
    for n in range(4):
        wb[n, :B, :B] = dot3(eb[0, n, :B, :B], element(di, n, 1))
        both = dot3(element(di, n, 0), element(lo, n, 0)) + dot3(wb[n, :B, :B], own(0, n))
        seg_out[2, n, :B, :B] = -both
    maps2 = send_maps(2)
    for k in (5, 6, 7):
        local[k].wait()
    arrived(halos)
    rows = right_sides(0)
    first, tails, heads = send_local(0, rows)
    arrived(maps0)
    p01 = dot3(seg(0, 1), seg(0, 0))
    p23 = dot3(seg(0, 3), seg(0, 2))
    part[0, :B, :B] = p01
    quarters = send_quarter(0, dot3(p23, p01))
    arrived(maps1)
    n01 = dot3(seg(1, 0), seg(1, 1))
    n23 = dot3(seg(1, 2), seg(1, 3))
    part[5, :B, :B] = n23
    quarters += send_quarter(1, dot3(n01, n23))
    arrived(maps2)
    k01 = seg(2, 0) + dot3(seg(1, 0), dot3(seg(2, 1), seg(0, 0)))
    k23 = seg(2, 2) + dot3(seg(1, 2), dot3(seg(2, 3), seg(0, 2)))
    quarters += send_quarter(2, k01 + dot3(n01, dot3(k23, p01)))
    arrived(first)
    starts, tail = quarter_tail(0)
    across, ends = send_quarter_vectors(0, starts, tail)
    p3 = dot3(seg(0, 2), p01)
    part[1, :B, :B] = p3
    k2 = dot3(seg(2, 3), p3)
    part[2, :B, :B] = k2
    k1 = dot3(seg(2, 2), p01) + dot3(seg(1, 2), k2)
    part[3, :B, :B] = k1
    part[4, :B, :B] = dot3(seg(2, 1), seg(0, 0)) + dot3(seg(1, 1), k1)
    part[6, :B, :B] = dot3(seg(1, 1), n23)
    arrived(quarters)
    arrived(across)
    back = send_entries(0, starts, ends)
    arrived(back)

    def keep(row, value):
        f8[row : row + 1, :] = value

    fields(0, tails, heads, keep)
    halos = send_halo(1, f8[...])
    arrived(halos)
    rows = right_sides(1)
    first, tails, heads = send_local(1, rows)
    arrived(first)
    starts, tail = quarter_tail(1)
    across, ends = send_quarter_vectors(1, starts, tail)
    arrived(across)
    back = send_entries(1, starts, ends)
    arrived(back)

    def give(row, value):
        out[row : row + 1, :] = value

    fields(1, tails, heads, give)
    for copy in sends:
        copy.wait_send()


def per_device(residual, previous, lower, pivot, upper, couple, restrict, neighbours):
    def factor(a):
        return jnp.transpose(a, (0, 2, 1, 3)).reshape(4, 2 * B, B)

    dma = pltpu.SemaphoreType.DMA
    result = pl.pallas_call(
        kernel,
        out_shape=jax.ShapeDtypeStruct((8, B), F32),
        in_specs=[pl.BlockSpec(memory_space=pl.ANY)] * 8,
        out_specs=pl.BlockSpec(memory_space=pltpu.VMEM),
        scratch_shapes=[
            pltpu.SMEM((4, 4), jnp.int32),
            pltpu.VMEM((8, B), F32),
            pltpu.VMEM((8, B), F32),
            pltpu.VMEM((Q, B), F32),
            pltpu.VMEM((4, 2 * B, B), F32),
            pltpu.VMEM((4, 2 * B, B), F32),
            pltpu.VMEM((4, 2 * B, B), F32),
            pltpu.VMEM((4, 2, Q, B), F32),
            pltpu.VMEM((2, 4, 104, 128), F32),
            pltpu.VMEM((4, 104, 128), F32),
            pltpu.VMEM((3, 4, 104, 128), F32),
            pltpu.VMEM((3, 4, 104, 128), F32),
            pltpu.VMEM((4, 3, 104, 128), F32),
            pltpu.VMEM((7, 104, 128), F32),
            pltpu.VMEM((12, 2, 256), F32),
            pltpu.VMEM((12, 2, 256), F32),
            pltpu.VMEM((8, Q), F32),
            pltpu.VMEM((8, B), F32),
            pltpu.VMEM((2, 4, 2, 128), F32),
            pltpu.VMEM((2, 4, 2, 128), F32),
            pltpu.VMEM((2, 4, 2, 128), F32),
            pltpu.VMEM((2, 4, 2, 128), F32),
            pltpu.VMEM((2, 4, 2, 128), F32),
            dma((8,)),
            dma((3, 3)),
            dma((3, 3)),
            dma((3, 3)),
            dma((3, 3)),
            dma((2, 2)),
            dma((2, 2)),
            dma((2, 3)),
            dma((2, 3)),
            dma((2, 3)),
            dma((2, 3)),
            dma((2, 3)),
            dma((2, 3)),
        ],
        compiler_params=pltpu.CompilerParams(
            collective_id=0, has_side_effects=True, vmem_limit_bytes=60 << 20
        ),
    )(
        neighbours,
        residual.reshape(8, B),
        previous.reshape(8, B),
        jnp.transpose(restrict, (1, 0, 2)).reshape(Q, B),
        factor(lower),
        factor(pivot),
        factor(upper),
        jnp.transpose(couple, (0, 1, 4, 2, 3)).reshape(4, 2, Q, B),
    )
    return result.reshape(4, 2, B)


def solution(mesh):
    placed = (
        P("patch", "line", None),
        P("patch", "line", None),
        P("patch", "line", None, None),
        P("patch", "line", None, None),
        P("patch", "line", None, None),
        P("patch", "line", None, None, None),
        P(),
        P("patch", None),
    )
    return jax.shard_map(
        per_device, mesh=mesh, in_specs=placed, out_specs=P("patch", "line", None), check_vma=False
    )
```

```python
import jax
import jax.numpy as jnp
from jax import lax
from jax.experimental import pallas as pl
from jax.experimental.pallas import tpu as pltpu
from jax.sharding import PartitionSpec as P

F32 = jnp.float32
BF16 = jnp.bfloat16
MESH = pl.DeviceIdType.MESH
B = 100
Q = 200
NP = 32
NN = (((1,), (0,)), ((), ()))
NT = (((1,), (1,)), ((), ()))


def split(a):
    high = a.astype(BF16)
    return high, (a - high.astype(F32)).astype(BF16)


def dot3(a, b, dims=NN):
    ah, al = split(a)
    bh, bl = split(b)

    def mm(u, v):
        return lax.dot_general(u, v, dims, preferred_element_type=F32)

    return mm(ah, bh) + (mm(ah, bl) + mm(al, bh))


def kernel(
    nb_any, res_any, prev_any, rst_any, low, piv, upp, fc, out,
    nb, res, prev, rst, lo, di, up, fo,
    eb, wb, seg_out, seg_in, quarter, part, hb_first, hb_second, lhs, f16, tr,
    a_out, a_in, th, fx, ob,
    s_loc, s_m, r_m, s_q, r_q, s_h, r_h, s_a, r_a, s_x, r_x, s_t, r_t, s_f, r_f,
):
    p = lax.axis_index("patch")
    line = lax.axis_index("line")
    x, y = line // 4, line % 4
    z, core = p // 2, p % 2
    ys = [(y + d) % 4 for d in range(4)]
    odd = core == 1

    def at(c, d, dz=0):
        return (((z + dz + NP // 2) % (NP // 2)) * 2 + c, x * 4 + ys[d])

    def x_peer(d):
        return (p, ((x + d) % 4) * 4 + y)

    def z_peer(d):
        return ((p + d + NP) % NP, line)

    def remote(src, dst, send, recv, device):
        return pltpu.make_async_remote_copy(
            src_ref=src, dst_ref=dst, send_sem=send, recv_sem=recv,
            device_id=device, device_id_type=MESH,
        )

    barrier = pltpu.get_barrier_semaphore()

    def greet(device):
        pl.semaphore_signal(barrier, inc=1, device_id=device, device_id_type=MESH)

    @pl.when(odd)
    def _():
        for d in (2, 1, 3):
            greet(at(1, d))
            greet(x_peer(d))
        greet(at(0, 0, 1))
        for d in (2, 1, 3, 0):
            greet(at(0, d))

    @pl.when(jnp.logical_not(odd))
    def _():
        for d in (2, 1, 3, 0):
            greet(at(1, d))
        greet(at(1, 0, -1))

    pairs = (
        (low, lo), (prev_any, prev), (rst_any, rst), (piv, di), (upp, up),
        (nb_any, nb), (res_any, res), (fc, fo),
    )
    local = [
        pltpu.make_async_copy(src, dst, s_loc.at[k]) for k, (src, dst) in enumerate(pairs)
    ]
    for copy in local:
        copy.start()

    hb = (hb_first, hb_second)
    sends = []
    sends_even = []
    sends_odd = []
    eye = lax.broadcasted_iota(jnp.int32, (B, B), 0) == lax.broadcasted_iota(
        jnp.int32, (B, B), 1
    )

    def to_row(column):
        return jnp.sum(jnp.where(eye, column, 0.0), axis=0, keepdims=True)

    def apply(matrix, row):
        return to_row(jnp.sum(matrix * row, axis=1, keepdims=True))

    def apply2(one, u, two, v):
        return to_row(jnp.sum(one * u + two * v, axis=1, keepdims=True))

    def element(ref, n, l):
        return ref[n, pl.ds(l, B, stride=2), :]

    def own(k, n):
        return seg_out[k, n, :B, :B]

    def to_owner(src, dst, send, recv):
        def make(d):
            return remote(src(ys[d]), dst(core, y), send.at[d], recv(core, d), at(1, d))

        for d in (2, 1, 3):
            make(d).start()
            sends.append(lambda d=d: make(d))

        @pl.when(jnp.logical_not(odd))
        def _():
            make(0).start()

        sends_even.append(lambda: make(0))

        @pl.when(odd)
        def _():
            dst(1, y)[...] = src(y)[...]

        def wait(d, c):
            remote(src(0), dst(c, 0), send.at[d], recv(c, d), at(1, 1)).wait_recv()

        def arrived():
            for d in (0, 1, 3, 2):
                wait(d, 0)
            for d in (1, 3, 2):
                wait(d, 1)

        return arrived

    def send_maps(k):
        return to_owner(
            lambda n: seg_out.at[k, n], lambda c, j: seg_in.at[c, k, j], s_m.at[k],
            lambda c, d: r_m.at[c, k, d],
        )

    lane = lax.broadcasted_iota(jnp.int32, (2, Q), 1) % 4

    def pick(block, source, f):
        total = jnp.zeros(block.shape, F32)
        for g in range(4):
            moved = block if g == f else pltpu.roll(block, (f - g) % 256, axis=1)
            total = jnp.where(source == g, moved, total)
        return jnp.where(lane == f, total[:, :Q], 0.0)

    def right_sides(sweep):
        for n in range(4):
            picked = jnp.zeros((2, Q), F32)
            for f in range(4):
                entry = nb[n, f]
                picked = picked + pick(
                    hb[sweep][(entry % 16) // 4, entry // 16], entry % 4, f
                )
            lhs[2 * n : 2 * n + 2, :] = picked
        whole = lhs[...]
        rows = []
        for row in range(8):
            got = dot3(whole, fo[row // 2, row % 2])
            rows.append(res[row : row + 1, :] - got[row : row + 1, :])
        return rows

    def send_local(sweep, rows):
        tails = []
        for n in range(4):
            tails.append(rows[2 * n + 1] - apply(element(lo, n, 1), rows[2 * n]))
        for n in range(4):
            a_out[sweep, n, 0:1, :B] = tails[n]
            a_out[sweep, n, 1:2, :B] = apply2(
                element(di, n, 0), rows[2 * n], wb[n, :B, :B], -tails[n]
            )
        return to_owner(
            lambda n: a_out.at[sweep, n], lambda c, j: a_in.at[sweep, c, j], s_a.at[sweep],
            lambda c, d: r_a.at[sweep, c, d],
        )

    both = (0, 1)

    def seg(c, k, j):
        return seg_in[c, k, j, :B, :B]

    def q(c, j, k):
        return quarter[j, k, c, :B, :B]

    def across(make):
        for d in (2, 1, 3):
            make(d).start()
            sends_odd.append(lambda d=d: make(d))

        def arrived():
            for d in (1, 3, 2):
                make(d).wait_recv()

        return arrived

    def send_quarter(k, values):
        for c in both:
            quarter[x, k, c, :B, :B] = values[c]
        return across(
            lambda d: remote(
                quarter.at[x, k], quarter.at[x, k], s_q.at[k, d], r_q.at[k, d], x_peer(d)
            )
        )

    def quarter_tails(sweep):
        tails = [[a_in[sweep, c, j, 0:1, :B] for j in range(4)] for c in both]
        y2 = [tails[c][1] + apply(seg(c, 0, 1), tails[c][0]) for c in both]
        y3 = [tails[c][2] + apply(seg(c, 0, 2), y2[c]) for c in both]
        last = [tails[c][3] + apply(seg(c, 0, 3), y3[c]) for c in both]
        return [(None, tails[c][0], y2[c], y3[c], last[c]) for c in both]

    def send_quarter_vectors(sweep, starts):
        heads = [[a_in[sweep, c, j, 1:2, :B] for j in range(4)] for c in both]
        ends = [[None, None, None, h[3]] for h in heads]
        g3 = [heads[c][3] + apply(seg(c, 2, 3), starts[c][3]) for c in both]
        g2 = [
            heads[c][2] + apply2(seg(c, 2, 2), starts[c][2], seg(c, 1, 2), g3[c]) for c in both
        ]
        g1 = [
            heads[c][1] + apply2(seg(c, 2, 1), starts[c][1], seg(c, 1, 1), g2[c]) for c in both
        ]
        g0 = [heads[c][0] + apply(seg(c, 1, 0), g1[c]) for c in both]
        for c in both:
            th[sweep, x, c, 0:1, :B] = starts[c][4]
            th[sweep, x, c, 1:2, :B] = g0[c]
        arrived = across(
            lambda d: remote(
                th.at[sweep, x], th.at[sweep, x], s_x.at[sweep, d], r_x.at[sweep, d], x_peer(d)
            )
        )
        return arrived, [(g0[c], g1[c], g2[c], g3[c]) for c in both]

    def mine(values):
        total = values[0]
        for j in range(1, 4):
            total = jnp.where(x == j, values[j], total)
        return total

    def fields(sweep, starts, ends):
        tail = [[th[sweep, j, c, 0:1, :B] for j in range(4)] for c in both]
        head = [[th[sweep, j, c, 1:2, :B] for j in range(4)] for c in both]
        zero = jnp.zeros((1, B), F32)
        y2 = [tail[c][1] + apply(q(c, 1, 0), tail[c][0]) for c in both]
        y3 = [tail[c][2] + apply(q(c, 2, 0), y2[c]) for c in both]
        h3 = [head[c][3] + apply(q(c, 3, 2), y3[c]) for c in both]
        h2 = [head[c][2] + apply2(q(c, 2, 2), y2[c], q(c, 2, 1), h3[c]) for c in both]
        h1 = [head[c][1] + apply2(q(c, 1, 2), tail[c][0], q(c, 1, 1), h2[c]) for c in both]
        result = []
        for c in both:
            y_in = mine((zero, tail[c][0], y2[c], y3[c]))
            x_in = mine((h1[c], h2[c], h3[c], zero))
            ahead = [
                starts[c][1] + apply(seg(c, 0, 0), y_in),
                starts[c][2] + apply(part[c, 0, :B, :B], y_in),
                starts[c][3] + apply(part[c, 1, :B, :B], y_in),
                starts[c][4] + apply(quarter[x, 0, c, :B, :B], y_in),
            ]
            g0, g1, g2, g3 = ends[c]
            first = [
                g0 + apply2(quarter[x, 2, c, :B, :B], y_in, quarter[x, 1, c, :B, :B], x_in),
                g1 + apply2(part[c, 4, :B, :B], y_in, part[c, 6, :B, :B], x_in),
                g2 + apply2(part[c, 3, :B, :B], y_in, part[c, 5, :B, :B], x_in),
                g3 + apply2(part[c, 2, :B, :B], y_in, seg(c, 1, 3), x_in),
            ]
            behind = first[1:] + [x_in]
            second = [
                apply2(seg(c, 3, j), ahead[j], seg(c, 4, j), -behind[j]) for j in range(4)
            ]
            result.append((first, second))
        return result

    local[0].wait()
    for n in range(4):
        seg_out[0, n, :B, :B] = dot3(element(lo, n, 1), element(lo, n, 0))
    local[1].wait()
    local[2].wait()
    halo = dot3(prev[...], rst[...], NT)
    for n in range(4):
        hb_first[n, 1, :, :Q] = halo[2 * n : 2 * n + 2]

    @pl.when(odd)
    def _():
        pl.semaphore_wait(barrier, 11)

    @pl.when(jnp.logical_not(odd))
    def _():
        pl.semaphore_wait(barrier, 5)

    halos = []
    for i, dp in enumerate((1, -1)):
        copy = remote(
            hb_first.at[:, 1], hb_first.at[:, 1 - dp], s_h.at[i], r_h.at[i], z_peer(dp)
        )
        copy.start()
        halos.append(copy)
        sends.append(lambda copy=copy: copy)
    maps0 = send_maps(0)
    local[3].wait()
    local[4].wait()
    for n in range(4):
        eb[n, :B, :B] = dot3(element(di, n, 0), element(up, n, 0))
        seg_out[4, n, :B, :B] = dot3(element(di, n, 1), element(up, n, 1))
        seg_out[1, n, :B, :B] = dot3(eb[n, :B, :B], own(4, n))
    maps1 = send_maps(1)
    for n in range(4):
        wb[n, :B, :B] = dot3(eb[n, :B, :B], element(di, n, 1))
        whole = dot3(element(di, n, 0), element(lo, n, 0)) + dot3(wb[n, :B, :B], own(0, n))
        seg_out[2, n, :B, :B] = -whole
    maps2 = send_maps(2)
    for n in range(4):
        seg_out[3, n, :B, :B] = element(di, n, 1)
    maps3 = send_maps(3)
    maps4 = send_maps(4)
    for k in (5, 6, 7):
        local[k].wait()
    for copy in halos:
        copy.wait_recv()
    first_in = send_local(0, right_sides(0))

    def send_traces(j, d):
        same = remote(
            tr.at[j], hb_second.at[y, pl.ds(1, 2)], s_t.at[0, d], r_t.at[0, d], at(0, d)
        )
        beside = remote(
            tr.at[j], hb_second.at[y, pl.ds(0, 2)], s_t.at[1, d], r_t.at[0, d], at(1, d)
        )
        below = remote(
            tr.at[j, 0], hb_second.at[y, 2], s_t.at[2, d], r_t.at[1, d], at(1, d, -1)
        )
        above = remote(
            tr.at[j, 1], hb_second.at[y, 0], s_t.at[3, d], r_t.at[1, d], at(0, d, 1)
        )
        return above, below, same, beside

    @pl.when(odd)
    def _():
        maps0()
        p01 = [dot3(seg(c, 0, 1), seg(c, 0, 0)) for c in both]
        p23 = [dot3(seg(c, 0, 3), seg(c, 0, 2)) for c in both]
        for c in both:
            part[c, 0, :B, :B] = p01[c]
        quarters0 = send_quarter(0, [dot3(p23[c], p01[c]) for c in both])
        maps1()
        n01 = [dot3(seg(c, 1, 0), seg(c, 1, 1)) for c in both]
        n23 = [dot3(seg(c, 1, 2), seg(c, 1, 3)) for c in both]
        for c in both:
            part[c, 5, :B, :B] = n23[c]
        quarters1 = send_quarter(1, [dot3(n01[c], n23[c]) for c in both])
        maps2()
        k1m0 = [dot3(seg(c, 2, 1), seg(c, 0, 0)) for c in both]
        k01 = [seg(c, 2, 0) + dot3(seg(c, 1, 0), k1m0[c]) for c in both]
        k23 = [
            seg(c, 2, 2) + dot3(seg(c, 1, 2), dot3(seg(c, 2, 3), seg(c, 0, 2))) for c in both
        ]
        quarters2 = send_quarter(
            2, [k01[c] + dot3(n01[c], dot3(k23[c], p01[c])) for c in both]
        )
        first_in()
        starts = quarter_tails(0)
        vectors, ends = send_quarter_vectors(0, starts)
        for c in both:
            p3 = dot3(seg(c, 0, 2), p01[c])
            part[c, 1, :B, :B] = p3
            k2 = dot3(seg(c, 2, 3), p3)
            part[c, 2, :B, :B] = k2
            k1 = dot3(seg(c, 2, 2), p01[c]) + dot3(seg(c, 1, 2), k2)
            part[c, 3, :B, :B] = k1
            part[c, 4, :B, :B] = k1m0[c] + dot3(seg(c, 1, 1), k1)
            part[c, 6, :B, :B] = dot3(seg(c, 1, 1), n23[c])
        maps3()
        maps4()
        quarters0()
        quarters1()
        quarters2()
        vectors()
        done = fields(0, starts, ends)
        for c in both:
            first, second = done[c]
            for j in range(4):
                row = 4 * j + 2 * c
                f16[row : row + 1, :] = first[j]
                f16[row + 1 : row + 2, :] = second[j]
        traces = dot3(f16[...], rst[...], NT)
        for j in range(4):
            for c in both:
                row = 4 * j + 2 * c
                tr[j, c, :, :Q] = traces[row : row + 2]
        for d in (2, 1, 3, 0):
            for copy in send_traces(ys[d], d)[: 4 if d else 3]:
                copy.start()
        hb_second[y, pl.ds(0, 2)] = tr[y]

    for d in range(4):
        send_traces(0, d)[0].wait_recv()

    for d in (1, 2, 3):
        send_traces(0, d)[3].wait_recv()

    @pl.when(jnp.logical_not(odd))
    def _():
        send_traces(0, 0)[3].wait_recv()

    second_in = send_local(1, right_sides(1))

    def send_field(d):
        even = remote(fx.at[ys[d], 0], ob.at[y], s_f.at[0, d], r_f.at[d], at(0, d))
        beside = remote(fx.at[ys[d], 1], ob.at[y], s_f.at[1, d], r_f.at[d], at(1, d))
        return even, beside

    @pl.when(odd)
    def _():
        second_in()
        starts = quarter_tails(1)
        vectors, ends = send_quarter_vectors(1, starts)
        vectors()
        done = fields(1, starts, ends)
        for c in both:
            first, second = done[c]
            for j in range(4):
                fx[j, c, 0:1, :B] = first[j]
                fx[j, c, 1:2, :B] = second[j]
        for d in (2, 1, 3, 0):
            for copy in send_field(d)[: 2 if d else 1]:
                copy.start()
        ob[y] = fx[y, 1]

    for d in (1, 2, 3):
        send_field(d)[0].wait_recv()

    @pl.when(jnp.logical_not(odd))
    def _():
        send_field(0)[0].wait_recv()

    for n in range(4):
        out[2 * n : 2 * n + 2, :] = ob[n, :, :B]
    for make in sends:
        make().wait_send()

    @pl.when(jnp.logical_not(odd))
    def _():
        for make in sends_even:
            make().wait_send()

    @pl.when(odd)
    def _():
        for make in sends_odd:
            make().wait_send()
        for d in range(4):
            for copy in send_traces(0, d)[: 4 if d else 3]:
                copy.wait_send()
            for copy in send_field(d)[: 2 if d else 1]:
                copy.wait_send()


def per_device(residual, previous, lower, pivot, upper, couple, restrict, neighbours):
    def factor(a):
        return jnp.transpose(a, (0, 2, 1, 3)).reshape(4, 2 * B, B)

    dma = pltpu.SemaphoreType.DMA
    result = pl.pallas_call(
        kernel,
        out_shape=jax.ShapeDtypeStruct((8, B), F32),
        in_specs=[pl.BlockSpec(memory_space=pl.ANY)] * 8,
        out_specs=pl.BlockSpec(memory_space=pltpu.VMEM),
        scratch_shapes=[
            pltpu.SMEM((4, 4), jnp.int32),
            pltpu.VMEM((8, B), F32),
            pltpu.VMEM((8, B), F32),
            pltpu.VMEM((Q, B), F32),
            pltpu.VMEM((4, 2 * B, B), F32),
            pltpu.VMEM((4, 2 * B, B), F32),
            pltpu.VMEM((4, 2 * B, B), F32),
            pltpu.VMEM((4, 2, Q, B), F32),
            pltpu.VMEM((4, 104, 128), F32),
            pltpu.VMEM((4, 104, 128), F32),
            pltpu.VMEM((5, 4, 104, 128), F32),
            pltpu.VMEM((2, 5, 4, 104, 128), F32),
            pltpu.VMEM((4, 3, 2, 104, 128), F32),
            pltpu.VMEM((2, 7, 104, 128), F32),
            pltpu.VMEM((4, 3, 2, 256), F32),
            pltpu.VMEM((4, 3, 2, 256), F32),
            pltpu.VMEM((8, Q), F32),
            pltpu.VMEM((16, B), F32),
            pltpu.VMEM((4, 2, 2, 256), F32),
            pltpu.VMEM((2, 4, 2, 128), F32),
            pltpu.VMEM((2, 2, 4, 2, 128), F32),
            pltpu.VMEM((2, 4, 2, 2, 128), F32),
            pltpu.VMEM((4, 2, 2, 128), F32),
            pltpu.VMEM((4, 2, 128), F32),
            dma((8,)),
            dma((5, 4)),
            dma((2, 5, 4)),
            dma((3, 4)),
            dma((3, 4)),
            dma((2,)),
            dma((2,)),
            dma((2, 4)),
            dma((2, 2, 4)),
            dma((2, 4)),
            dma((2, 4)),
            dma((4, 4)),
            dma((2, 4)),
            dma((2, 4)),
            dma((4,)),
        ],
        compiler_params=pltpu.CompilerParams(
            collective_id=0, has_side_effects=True, vmem_limit_bytes=60 << 20
        ),
    )(
        neighbours,
        residual.reshape(8, B),
        previous.reshape(8, B),
        jnp.transpose(restrict, (1, 0, 2)).reshape(Q, B),
        factor(lower),
        factor(pivot),
        factor(upper),
        jnp.transpose(couple, (0, 1, 4, 2, 3)).reshape(4, 2, Q, B),
    )
    return result.reshape(4, 2, B)


def solution(mesh):
    placed = (
        P("patch", "line", None),
        P("patch", "line", None),
        P("patch", "line", None, None),
        P("patch", "line", None, None),
        P("patch", "line", None, None),
        P("patch", "line", None, None, None),
        P(),
        P("patch", None),
    )
    return jax.shard_map(
        per_device, mesh=mesh, in_specs=placed, out_specs=P("patch", "line", None), check_vma=False
    )
```

```python
import jax
import jax.numpy as jnp
from jax import lax
from jax.experimental import pallas as pl
from jax.experimental.pallas import tpu as pltpu
from jax.sharding import PartitionSpec as P

F32 = jnp.float32
BF16 = jnp.bfloat16
MESH = pl.DeviceIdType.MESH
B = 100
Q = 200
NP = 32
NN = (((1,), (0,)), ((), ()))
NT = (((1,), (1,)), ((), ()))


def split(a):
    high = a.astype(BF16)
    return high, (a - high.astype(F32)).astype(BF16)


def dot3(a, b, dims=NN):
    ah, al = split(a)
    bh, bl = split(b)

    def mm(u, v):
        return lax.dot_general(u, v, dims, preferred_element_type=F32)

    return mm(ah, bh) + (mm(ah, bl) + mm(al, bh))


def kernel(
    nb_any, res_any, prev_any, rst_any, low, piv, upp, fc, out,
    nb, res, prev, rst, lo, di, up, fo,
    eb, wb, seg_out, seg_in, quarter, part, de, hb_first, hb_second, lhs, f24, ent_out, ent_in,
    a_out, a_in, th, fx, ob,
    s_loc, s_d, r_d, s_m, r_m, s_q, r_q, s_h, r_h, s_a, r_a, s_x, r_x, s_t, r_t, s_f, r_f,
):
    p = lax.axis_index("patch")
    line = lax.axis_index("line")
    x, y = line // 4, line % 4
    z, core = p // 2, p % 2
    ys = [(y + d) % 4 for d in range(4)]
    odd = core == 1

    def at(c, d, dz=0):
        return (((z + dz + NP // 2) % (NP // 2)) * 2 + c, x * 4 + ys[d])

    def x_peer(d):
        return (p, ((x + d) % 4) * 4 + y)

    def z_peer(d):
        return ((p + d + NP) % NP, line)

    def remote(src, dst, send, recv, device):
        return pltpu.make_async_remote_copy(
            src_ref=src, dst_ref=dst, send_sem=send, recv_sem=recv,
            device_id=device, device_id_type=MESH,
        )

    barrier = pltpu.get_barrier_semaphore()

    def greet(device):
        pl.semaphore_signal(barrier, inc=1, device_id=device, device_id_type=MESH)

    @pl.when(odd)
    def _():
        for d in (2, 1, 3):
            greet(at(1, d))
            greet(x_peer(d))
        greet(at(0, 0, 1))
        for d in (2, 1, 3, 0):
            greet(at(0, d))

    @pl.when(jnp.logical_not(odd))
    def _():
        for d in (2, 1, 3, 0):
            greet(at(1, d))
        greet(at(1, 0, -1))

    pairs = (
        (low, lo), (prev_any, prev), (rst_any, rst), (piv, di), (upp, up),
        (nb_any, nb), (res_any, res), (fc, fo),
    )
    local = [
        pltpu.make_async_copy(src, dst, s_loc.at[k]) for k, (src, dst) in enumerate(pairs)
    ]
    for copy in local:
        copy.start()

    hb = (hb_first, hb_second)
    sends = []
    sends_even = []
    sends_odd = []
    eye = lax.broadcasted_iota(jnp.int32, (B, B), 0) == lax.broadcasted_iota(
        jnp.int32, (B, B), 1
    )

    def to_row(column):
        return jnp.sum(jnp.where(eye, column, 0.0), axis=0, keepdims=True)

    def apply(matrix, row):
        return to_row(jnp.sum(matrix * row, axis=1, keepdims=True))

    def apply2(one, u, two, v):
        return to_row(jnp.sum(one * u + two * v, axis=1, keepdims=True))

    def element(ref, n, l):
        return ref[n, pl.ds(l, B, stride=2), :]

    def own(k, n):
        return seg_out[k, n, :B, :B]

    def to_owner(src, dst, send, recv):
        def make(d):
            return remote(src(ys[d]), dst(core, y), send.at[d], recv(core, d), at(1, d))

        for d in (2, 1, 3):
            make(d).start()
            sends.append(lambda d=d: make(d))

        @pl.when(jnp.logical_not(odd))
        def _():
            make(0).start()

        sends_even.append(lambda: make(0))

        @pl.when(odd)
        def _():
            dst(1, y)[...] = src(y)[...]

        def wait(d, c):
            remote(src(0), dst(c, 0), send.at[d], recv(c, d), at(1, 1)).wait_recv()

        def arrived():
            for d in (0, 1, 3, 2):
                wait(d, 0)
            for d in (1, 3, 2):
                wait(d, 1)

        return arrived

    def send_maps(k):
        return to_owner(
            lambda n: seg_out.at[k, n], lambda c, j: seg_in.at[c, k, j], s_m.at[k],
            lambda c, d: r_m.at[c, k, d],
        )

    lane = lax.broadcasted_iota(jnp.int32, (2, Q), 1) % 4

    def pick(block, source, f):
        total = jnp.zeros(block.shape, F32)
        for g in range(4):
            moved = block if g == f else pltpu.roll(block, (f - g) % 256, axis=1)
            total = jnp.where(source == g, moved, total)
        return jnp.where(lane == f, total[:, :Q], 0.0)

    def right_sides(sweep):
        for n in range(4):
            picked = jnp.zeros((2, Q), F32)
            for f in range(4):
                entry = nb[n, f]
                picked = picked + pick(
                    hb[sweep][entry // 4], entry % 4, f
                )
            lhs[2 * n : 2 * n + 2, :] = picked
        whole = lhs[...]
        rows = []
        for row in range(8):
            got = dot3(whole, fo[row // 2, row % 2])
            rows.append(res[row : row + 1, :] - got[row : row + 1, :])
        return rows

    def send_local(sweep, rows):
        tails = []
        for n in range(4):
            tails.append(rows[2 * n + 1] - apply(element(lo, n, 1), rows[2 * n]))
        for n in range(4):
            a_out[sweep, n, 0:1, :B] = tails[n]
            a_out[sweep, n, 1:2, :B] = apply2(
                element(di, n, 0), rows[2 * n], wb[n, :B, :B], -tails[n]
            )
        return to_owner(
            lambda n: a_out.at[sweep, n], lambda c, j: a_in.at[sweep, c, j], s_a.at[sweep],
            lambda c, d: r_a.at[sweep, c, d],
        )

    both = (0, 1)

    def seg(c, k, j):
        return seg_in[c, k, j, :B, :B]

    def q(c, j, k):
        return quarter[j, k, c, :B, :B]

    def across(make):
        for d in (2, 1, 3):
            make(d).start()
            sends_odd.append(lambda d=d: make(d))

        def arrived():
            for d in (1, 3, 2):
                make(d).wait_recv()

        return arrived

    def send_quarter(k, values):
        for c in both:
            quarter[x, k, c, :B, :B] = values[c]
        return across(
            lambda d: remote(
                quarter.at[x, k], quarter.at[x, k], s_q.at[k, d], r_q.at[k, d], x_peer(d)
            )
        )

    def quarter_tails(sweep):
        tails = [[a_in[sweep, c, j, 0:1, :B] for j in range(4)] for c in both]
        y2 = [tails[c][1] + apply(seg(c, 0, 1), tails[c][0]) for c in both]
        y3 = [tails[c][2] + apply(seg(c, 0, 2), y2[c]) for c in both]
        last = [tails[c][3] + apply(seg(c, 0, 3), y3[c]) for c in both]
        return [(None, tails[c][0], y2[c], y3[c], last[c]) for c in both]

    def send_quarter_vectors(sweep, starts):
        heads = [[a_in[sweep, c, j, 1:2, :B] for j in range(4)] for c in both]
        ends = [[None, None, None, h[3]] for h in heads]
        g3 = [heads[c][3] + apply(seg(c, 2, 3), starts[c][3]) for c in both]
        g2 = [
            heads[c][2] + apply2(seg(c, 2, 2), starts[c][2], seg(c, 1, 2), g3[c]) for c in both
        ]
        g1 = [
            heads[c][1] + apply2(seg(c, 2, 1), starts[c][1], seg(c, 1, 1), g2[c]) for c in both
        ]
        g0 = [heads[c][0] + apply(seg(c, 1, 0), g1[c]) for c in both]
        for c in both:
            th[sweep, x, c, 0:1, :B] = starts[c][4]
            th[sweep, x, c, 1:2, :B] = g0[c]
        arrived = across(
            lambda d: remote(
                th.at[sweep, x], th.at[sweep, x], s_x.at[sweep, d], r_x.at[sweep, d], x_peer(d)
            )
        )
        return arrived, [(g0[c], g1[c], g2[c], g3[c]) for c in both]

    def mine(values):
        total = values[0]
        for j in range(1, 4):
            total = jnp.where(x == j, values[j], total)
        return total

    def fields(sweep, starts, ends):
        tail = [[th[sweep, j, c, 0:1, :B] for j in range(4)] for c in both]
        head = [[th[sweep, j, c, 1:2, :B] for j in range(4)] for c in both]
        zero = jnp.zeros((1, B), F32)
        y2 = [tail[c][1] + apply(q(c, 1, 0), tail[c][0]) for c in both]
        y3 = [tail[c][2] + apply(q(c, 2, 0), y2[c]) for c in both]
        h3 = [head[c][3] + apply(q(c, 3, 2), y3[c]) for c in both]
        h2 = [head[c][2] + apply2(q(c, 2, 2), y2[c], q(c, 2, 1), h3[c]) for c in both]
        h1 = [head[c][1] + apply2(q(c, 1, 2), tail[c][0], q(c, 1, 1), h2[c]) for c in both]
        result = []
        for c in both:
            y_in = mine((zero, tail[c][0], y2[c], y3[c]))
            x_in = mine((h1[c], h2[c], h3[c], zero))
            ahead = [
                starts[c][1] + apply(seg(c, 0, 0), y_in),
                starts[c][2] + apply(part[c, 0, :B, :B], y_in),
                starts[c][3] + apply(part[c, 1, :B, :B], y_in),
                starts[c][4] + apply(quarter[x, 0, c, :B, :B], y_in),
            ]
            g0, g1, g2, g3 = ends[c]
            first = [
                g0 + apply2(quarter[x, 2, c, :B, :B], y_in, quarter[x, 1, c, :B, :B], x_in),
                g1 + apply2(part[c, 4, :B, :B], y_in, part[c, 6, :B, :B], x_in),
                g2 + apply2(part[c, 3, :B, :B], y_in, part[c, 5, :B, :B], x_in),
                g3 + apply2(part[c, 2, :B, :B], y_in, seg(c, 1, 3), x_in),
            ]
            behind = first[1:] + [x_in]
            result.append((first, ahead, behind))
        return result

    local[0].wait()
    for n in range(4):
        seg_out[0, n, :B, :B] = dot3(element(lo, n, 1), element(lo, n, 0))
    local[1].wait()
    local[2].wait()
    halo = dot3(prev[...], rst[...], NT)
    for n in range(4):
        hb_first[4 + n, :, :Q] = halo[2 * n : 2 * n + 2]

    @pl.when(odd)
    def _():
        pl.semaphore_wait(barrier, 11)

    @pl.when(jnp.logical_not(odd))
    def _():
        pl.semaphore_wait(barrier, 5)

    halos = []
    for i, dp in enumerate((1, -1)):
        copy = remote(
            hb_first.at[pl.ds(4, 4)], hb_first.at[pl.ds((1 - dp) * 4, 4)], s_h.at[i], r_h.at[i],
            z_peer(dp),
        )
        copy.start()
        halos.append(copy)
        sends.append(lambda copy=copy: copy)
    maps0 = send_maps(0)
    local[3].wait()
    local[4].wait()
    for n in range(4):
        eb[n, :B, :B] = dot3(element(di, n, 0), element(up, n, 0))
        seg_out[4, n, :B, :B] = dot3(element(di, n, 1), element(up, n, 1))
        seg_out[1, n, :B, :B] = dot3(eb[n, :B, :B], own(4, n))
    maps1 = send_maps(1)
    for n in range(4):
        wb[n, :B, :B] = dot3(eb[n, :B, :B], element(di, n, 1))
        whole = dot3(element(di, n, 0), element(lo, n, 0)) + dot3(wb[n, :B, :B], own(0, n))
        seg_out[2, n, :B, :B] = -whole
    maps2 = send_maps(2)
    for n in range(4):
        seg_out[3, n, :B, :B] = element(di, n, 1)
    beside = []
    for i, dp in enumerate((1, -1)):
        copy = remote(
            seg_out.at[pl.ds(3, 2)], de.at[1 - dp], s_d.at[i], r_d.at[i], z_peer(dp)
        )
        copy.start()
        beside.append(copy)
        sends.append(lambda copy=copy: copy)
    for k in (5, 6, 7):
        local[k].wait()
    for copy in halos:
        copy.wait_recv()
    first_in = send_local(0, right_sides(0))
    def send_entries(j, d):
        same = remote(
            ent_out.at[j], ent_in.at[y, pl.ds(1, 2)], s_t.at[0, d], r_t.at[0, d], at(0, d)
        )
        beside = remote(
            ent_out.at[j], ent_in.at[y, pl.ds(0, 2)], s_t.at[1, d], r_t.at[0, d], at(1, d)
        )
        below = remote(
            ent_out.at[j, 0], ent_in.at[y, 2], s_t.at[2, d], r_t.at[1, d], at(1, d, -1)
        )
        above = remote(
            ent_out.at[j, 1], ent_in.at[y, 0], s_t.at[3, d], r_t.at[1, d], at(0, d, 1)
        )
        return above, below, same, beside

    def store_entries(ref, done):
        for c in both:
            for j in range(4):
                for row in range(3):
                    ref[j, c, row : row + 1, :B] = done[c][row][j]

    @pl.when(odd)
    def _():
        maps0()
        p01 = [dot3(seg(c, 0, 1), seg(c, 0, 0)) for c in both]
        p23 = [dot3(seg(c, 0, 3), seg(c, 0, 2)) for c in both]
        for c in both:
            part[c, 0, :B, :B] = p01[c]
        quarters0 = send_quarter(0, [dot3(p23[c], p01[c]) for c in both])
        maps1()
        n01 = [dot3(seg(c, 1, 0), seg(c, 1, 1)) for c in both]
        n23 = [dot3(seg(c, 1, 2), seg(c, 1, 3)) for c in both]
        for c in both:
            part[c, 5, :B, :B] = n23[c]
        quarters1 = send_quarter(1, [dot3(n01[c], n23[c]) for c in both])
        maps2()
        k1m0 = [dot3(seg(c, 2, 1), seg(c, 0, 0)) for c in both]
        k01 = [seg(c, 2, 0) + dot3(seg(c, 1, 0), k1m0[c]) for c in both]
        k23 = [
            seg(c, 2, 2) + dot3(seg(c, 1, 2), dot3(seg(c, 2, 3), seg(c, 0, 2))) for c in both
        ]
        quarters2 = send_quarter(
            2, [k01[c] + dot3(n01[c], dot3(k23[c], p01[c])) for c in both]
        )
        first_in()
        starts = quarter_tails(0)
        vectors, ends = send_quarter_vectors(0, starts)
        for c in both:
            p3 = dot3(seg(c, 0, 2), p01[c])
            part[c, 1, :B, :B] = p3
            k2 = dot3(seg(c, 2, 3), p3)
            part[c, 2, :B, :B] = k2
            k1 = dot3(seg(c, 2, 2), p01[c]) + dot3(seg(c, 1, 2), k2)
            part[c, 3, :B, :B] = k1
            part[c, 4, :B, :B] = k1m0[c] + dot3(seg(c, 1, 1), k1)
            part[c, 6, :B, :B] = dot3(seg(c, 1, 1), n23[c])
        quarters0()
        quarters1()
        quarters2()
        vectors()
        done = fields(0, starts, ends)
        store_entries(ent_out, done)
        for d in (2, 1, 3, 0):
            for copy in send_entries(ys[d], d)[: 4 if d else 3]:
                copy.start()
        ent_in[y, pl.ds(0, 2)] = ent_out[y]

    for copy in beside:
        copy.wait_recv()
    for d in range(4):
        send_entries(0, d)[0].wait_recv()

    for d in (1, 2, 3):
        send_entries(0, d)[3].wait_recv()

    @pl.when(jnp.logical_not(odd))
    def _():
        send_entries(0, 0)[3].wait_recv()

    for o in range(3):
        for n in range(4):
            row = 8 * o + 2 * n
            entry = ent_in[n, o]
            if o == 1:
                pivot, upper = own(3, n), own(4, n)
            else:
                pivot, upper = de[o, 0, n, :B, :B], de[o, 1, n, :B, :B]
            f24[row : row + 1, :] = entry[0:1, :B]
            f24[row + 1 : row + 2, :] = apply2(pivot, entry[1:2, :B], upper, -entry[2:3, :B])
    halo = dot3(f24[...], rst[...], NT)
    for m in range(12):
        hb_second[m, :, :Q] = halo[2 * m : 2 * m + 2]
    second_in = send_local(1, right_sides(1))

    def send_field(d):
        even = remote(fx.at[ys[d], 0], ob.at[y], s_f.at[0, d], r_f.at[d], at(0, d))
        beside = remote(fx.at[ys[d], 1], ob.at[y], s_f.at[1, d], r_f.at[d], at(1, d))
        return even, beside

    @pl.when(odd)
    def _():
        second_in()
        starts = quarter_tails(1)
        vectors, ends = send_quarter_vectors(1, starts)
        vectors()
        done = fields(1, starts, ends)
        store_entries(fx, done)
        for d in (2, 1, 3, 0):
            for copy in send_field(d)[: 2 if d else 1]:
                copy.start()
        ob[y] = fx[y, 1]

    for d in (1, 2, 3):
        send_field(d)[0].wait_recv()

    @pl.when(jnp.logical_not(odd))
    def _():
        send_field(0)[0].wait_recv()

    for n in range(4):
        entry = ob[n]
        out[2 * n : 2 * n + 1, :] = entry[0:1, :B]
        out[2 * n + 1 : 2 * n + 2, :] = apply2(
            own(3, n), entry[1:2, :B], own(4, n), -entry[2:3, :B]
        )
    for make in sends:
        make().wait_send()

    @pl.when(jnp.logical_not(odd))
    def _():
        for make in sends_even:
            make().wait_send()

    @pl.when(odd)
    def _():
        for make in sends_odd:
            make().wait_send()
        for d in range(4):
            for copy in send_entries(0, d)[: 4 if d else 3]:
                copy.wait_send()
            for copy in send_field(d)[: 2 if d else 1]:
                copy.wait_send()


def per_device(residual, previous, lower, pivot, upper, couple, restrict, neighbours):
    def factor(a):
        return jnp.transpose(a, (0, 2, 1, 3)).reshape(4, 2 * B, B)

    dma = pltpu.SemaphoreType.DMA
    result = pl.pallas_call(
        kernel,
        out_shape=jax.ShapeDtypeStruct((8, B), F32),
        in_specs=[pl.BlockSpec(memory_space=pl.ANY)] * 8,
        out_specs=pl.BlockSpec(memory_space=pltpu.VMEM),
        scratch_shapes=[
            pltpu.SMEM((4, 4), jnp.int32),
            pltpu.VMEM((8, B), F32),
            pltpu.VMEM((8, B), F32),
            pltpu.VMEM((Q, B), F32),
            pltpu.VMEM((4, 2 * B, B), F32),
            pltpu.VMEM((4, 2 * B, B), F32),
            pltpu.VMEM((4, 2 * B, B), F32),
            pltpu.VMEM((4, 2, Q, B), F32),
            pltpu.VMEM((4, 104, 128), F32),
            pltpu.VMEM((4, 104, 128), F32),
            pltpu.VMEM((5, 4, 104, 128), F32),
            pltpu.VMEM((2, 3, 4, 104, 128), F32),
            pltpu.VMEM((4, 3, 2, 104, 128), F32),
            pltpu.VMEM((2, 7, 104, 128), F32),
            pltpu.VMEM((3, 2, 4, 104, 128), F32),
            pltpu.VMEM((12, 2, 256), F32),
            pltpu.VMEM((12, 2, 256), F32),
            pltpu.VMEM((8, Q), F32),
            pltpu.VMEM((24, B), F32),
            pltpu.VMEM((4, 2, 4, 128), F32),
            pltpu.VMEM((4, 3, 4, 128), F32),
            pltpu.VMEM((2, 4, 2, 128), F32),
            pltpu.VMEM((2, 2, 4, 2, 128), F32),
            pltpu.VMEM((2, 4, 2, 2, 128), F32),
            pltpu.VMEM((4, 2, 4, 128), F32),
            pltpu.VMEM((4, 4, 128), F32),
            dma((8,)),
            dma((2,)),
            dma((2,)),
            dma((3, 4)),
            dma((2, 3, 4)),
            dma((3, 4)),
            dma((3, 4)),
            dma((2,)),
            dma((2,)),
            dma((2, 4)),
            dma((2, 2, 4)),
            dma((2, 4)),
            dma((2, 4)),
            dma((4, 4)),
            dma((2, 4)),
            dma((2, 4)),
            dma((4,)),
        ],
        compiler_params=pltpu.CompilerParams(
            collective_id=0, has_side_effects=True, vmem_limit_bytes=60 << 20
        ),
    )(
        neighbours,
        residual.reshape(8, B),
        previous.reshape(8, B),
        jnp.transpose(restrict, (1, 0, 2)).reshape(Q, B),
        factor(lower),
        factor(pivot),
        factor(upper),
        jnp.transpose(couple, (0, 1, 4, 2, 3)).reshape(4, 2, Q, B),
    )
    return result.reshape(4, 2, B)


def solution(mesh):
    placed = (
        P("patch", "line", None),
        P("patch", "line", None),
        P("patch", "line", None, None),
        P("patch", "line", None, None),
        P("patch", "line", None, None),
        P("patch", "line", None, None, None),
        P(),
        P("patch", None),
    )
    return jax.shard_map(
        per_device, mesh=mesh, in_specs=placed, out_specs=P("patch", "line", None), check_vma=False
    )
```

```python
import jax
import jax.numpy as jnp
from jax import lax
from jax.experimental import pallas as pl
from jax.experimental.pallas import tpu as pltpu
from jax.sharding import PartitionSpec as P

F32 = jnp.float32
BF16 = jnp.bfloat16
MESH = pl.DeviceIdType.MESH
B = 100
Q = 200
NP = 32
NN = (((1,), (0,)), ((), ()))
NT = (((1,), (1,)), ((), ()))


def split(a):
    high = a.astype(BF16)
    return high, (a - high.astype(F32)).astype(BF16)


def dot3(a, b, dims=NN):
    ah, al = split(a)
    bh, bl = split(b)

    def mm(u, v):
        return lax.dot_general(u, v, dims, preferred_element_type=F32)

    return mm(ah, bh) + (mm(ah, bl) + mm(al, bh))


def kernel(
    nb_any, res_any, prev_any, rst_any, low, piv, upp, fc, out,
    nb, res, prev, rst, lo, di, up, fo,
    eb, wb, seg_out, seg_in, quarter, part, de, hb_first, hb_second, lhs, f24, ent_out, ent_in,
    a_out, a_in, th, fx, ob,
    s_loc, s_d, r_d, s_m, r_m, s_q, r_q, s_h, r_h, s_a, r_a, s_x, r_x, s_t, r_t, s_f, r_f,
):
    p = lax.axis_index("patch")
    line = lax.axis_index("line")
    x, y = line // 4, line % 4
    z, core = p // 2, p % 2
    ys = [(y + d) % 4 for d in range(4)]
    odd = core == 1

    def at(c, d, dz=0):
        return (((z + dz + NP // 2) % (NP // 2)) * 2 + c, x * 4 + ys[d])

    def x_peer(d):
        return (p, ((x + d) % 4) * 4 + y)

    def z_peer(d):
        return ((p + d + NP) % NP, line)

    def remote(src, dst, send, recv, device):
        return pltpu.make_async_remote_copy(
            src_ref=src, dst_ref=dst, send_sem=send, recv_sem=recv,
            device_id=device, device_id_type=MESH,
        )

    barrier = pltpu.get_barrier_semaphore()

    def greet(device):
        pl.semaphore_signal(barrier, inc=1, device_id=device, device_id_type=MESH)

    @pl.when(odd)
    def _():
        for d in (2, 1, 3):
            greet(at(1, d))
            greet(x_peer(d))
        greet(at(0, 0, 1))
        for d in (2, 1, 3, 0):
            greet(at(0, d))

    pairs = (
        (low, lo), (prev_any, prev), (rst_any, rst), (piv, di), (upp, up),
        (nb_any, nb), (res_any, res), (fc, fo),
    )
    local = [
        pltpu.make_async_copy(src, dst, s_loc.at[k]) for k, (src, dst) in enumerate(pairs)
    ]
    for copy in local:
        copy.start()

    hb = (hb_first, hb_second)
    sends = []
    sends_even = []
    sends_odd = []
    eye = lax.broadcasted_iota(jnp.int32, (B, B), 0) == lax.broadcasted_iota(
        jnp.int32, (B, B), 1
    )

    def to_row(column):
        return jnp.sum(jnp.where(eye, column, 0.0), axis=0, keepdims=True)

    def apply(matrix, row):
        return to_row(jnp.sum(matrix * row, axis=1, keepdims=True))

    def apply2(one, u, two, v):
        return to_row(jnp.sum(one * u + two * v, axis=1, keepdims=True))

    def element(ref, n, l):
        return ref[n, pl.ds(l, B, stride=2), :]

    def own(k, n):
        return seg_out[k, n, :B, :B]

    def to_owner(src, dst, send, recv):
        def make(d):
            return remote(src(ys[d]), dst(core, y), send.at[d], recv(core, d), at(1, d))

        for d in (2, 1, 3):
            make(d).start()
            sends.append(lambda d=d: make(d))

        @pl.when(jnp.logical_not(odd))
        def _():
            make(0).start()

        sends_even.append(lambda: make(0))

        @pl.when(odd)
        def _():
            dst(1, y)[...] = src(y)[...]

        def wait(d, c):
            remote(src(0), dst(c, 0), send.at[d], recv(c, d), at(1, 1)).wait_recv()

        def arrived():
            for d in (0, 1, 3, 2):
                wait(d, 0)
            for d in (1, 3, 2):
                wait(d, 1)

        return arrived

    def send_maps(k):
        return to_owner(
            lambda n: seg_out.at[k, n], lambda c, j: seg_in.at[c, k, j], s_m.at[k],
            lambda c, d: r_m.at[c, k, d],
        )

    lane = lax.broadcasted_iota(jnp.int32, (2, Q), 1) % 4

    def pick(block, source, f):
        total = jnp.zeros(block.shape, F32)
        for g in range(4):
            moved = block if g == f else pltpu.roll(block, (f - g) % 256, axis=1)
            total = jnp.where(source == g, moved, total)
        return jnp.where(lane == f, total[:, :Q], 0.0)

    def right_sides(sweep):
        for n in range(4):
            picked = jnp.zeros((2, Q), F32)
            for f in range(4):
                entry = nb[n, f]
                picked = picked + pick(
                    hb[sweep][entry // 4], entry % 4, f
                )
            lhs[2 * n : 2 * n + 2, :] = picked
        whole = lhs[...]
        rows = []
        for row in range(8):
            got = dot3(whole, fo[row // 2, row % 2])
            rows.append(res[row : row + 1, :] - got[row : row + 1, :])
        return rows

    def send_local(sweep, rows):
        tails = []
        for n in range(4):
            tails.append(rows[2 * n + 1] - apply(element(lo, n, 1), rows[2 * n]))
        for n in range(4):
            a_out[sweep, n, 0:1, :B] = tails[n]
            a_out[sweep, n, 1:2, :B] = apply2(
                element(di, n, 0), rows[2 * n], wb[n, :B, :B], -tails[n]
            )
        return to_owner(
            lambda n: a_out.at[sweep, n], lambda c, j: a_in.at[sweep, c, j], s_a.at[sweep],
            lambda c, d: r_a.at[sweep, c, d],
        )

    both = (0, 1)

    def seg(c, k, j):
        return seg_in[c, k, j, :B, :B]

    def q(c, j, k):
        return quarter[j, k, c, :B, :B]

    def across(make):
        for d in (2, 1, 3):
            make(d).start()
            sends_odd.append(lambda d=d: make(d))

        def arrived():
            for d in (1, 3, 2):
                make(d).wait_recv()

        return arrived

    def send_quarter(k, values):
        for c in both:
            quarter[x, k, c, :B, :B] = values[c]
        return across(
            lambda d: remote(
                quarter.at[x, k], quarter.at[x, k], s_q.at[k, d], r_q.at[k, d], x_peer(d)
            )
        )

    def quarter_tails(sweep):
        tails = [[a_in[sweep, c, j, 0:1, :B] for j in range(4)] for c in both]
        y2 = [tails[c][1] + apply(seg(c, 0, 1), tails[c][0]) for c in both]
        y3 = [tails[c][2] + apply(seg(c, 0, 2), y2[c]) for c in both]
        last = [tails[c][3] + apply(seg(c, 0, 3), y3[c]) for c in both]
        return [(None, tails[c][0], y2[c], y3[c], last[c]) for c in both]

    def send_quarter_vectors(sweep, starts):
        heads = [[a_in[sweep, c, j, 1:2, :B] for j in range(4)] for c in both]
        ends = [[None, None, None, h[3]] for h in heads]
        g3 = [heads[c][3] + apply(seg(c, 2, 3), starts[c][3]) for c in both]
        g2 = [
            heads[c][2] + apply2(seg(c, 2, 2), starts[c][2], seg(c, 1, 2), g3[c]) for c in both
        ]
        g1 = [
            heads[c][1] + apply2(seg(c, 2, 1), starts[c][1], seg(c, 1, 1), g2[c]) for c in both
        ]
        g0 = [heads[c][0] + apply(seg(c, 1, 0), g1[c]) for c in both]
        for c in both:
            th[sweep, x, c, 0:1, :B] = starts[c][4]
            th[sweep, x, c, 1:2, :B] = g0[c]
        arrived = across(
            lambda d: remote(
                th.at[sweep, x], th.at[sweep, x], s_x.at[sweep, d], r_x.at[sweep, d], x_peer(d)
            )
        )
        return arrived, [(g0[c], g1[c], g2[c], g3[c]) for c in both]

    def mine(values):
        total = values[0]
        for j in range(1, 4):
            total = jnp.where(x == j, values[j], total)
        return total

    def fields(sweep, starts, ends):
        tail = [[th[sweep, j, c, 0:1, :B] for j in range(4)] for c in both]
        head = [[th[sweep, j, c, 1:2, :B] for j in range(4)] for c in both]
        zero = jnp.zeros((1, B), F32)
        y2 = [tail[c][1] + apply(q(c, 1, 0), tail[c][0]) for c in both]
        y3 = [tail[c][2] + apply(q(c, 2, 0), y2[c]) for c in both]
        h3 = [head[c][3] + apply(q(c, 3, 2), y3[c]) for c in both]
        h2 = [head[c][2] + apply2(q(c, 2, 2), y2[c], q(c, 2, 1), h3[c]) for c in both]
        h1 = [head[c][1] + apply2(q(c, 1, 2), tail[c][0], q(c, 1, 1), h2[c]) for c in both]
        result = []
        for c in both:
            y_in = mine((zero, tail[c][0], y2[c], y3[c]))
            x_in = mine((h1[c], h2[c], h3[c], zero))
            ahead = [
                starts[c][1] + apply(seg(c, 0, 0), y_in),
                starts[c][2] + apply(part[c, 0, :B, :B], y_in),
                starts[c][3] + apply(part[c, 1, :B, :B], y_in),
                starts[c][4] + apply(quarter[x, 0, c, :B, :B], y_in),
            ]
            g0, g1, g2, g3 = ends[c]
            first = [
                g0 + apply2(quarter[x, 2, c, :B, :B], y_in, quarter[x, 1, c, :B, :B], x_in),
                g1 + apply2(part[c, 4, :B, :B], y_in, part[c, 6, :B, :B], x_in),
                g2 + apply2(part[c, 3, :B, :B], y_in, part[c, 5, :B, :B], x_in),
                g3 + apply2(part[c, 2, :B, :B], y_in, seg(c, 1, 3), x_in),
            ]
            behind = first[1:] + [x_in]
            result.append((first, ahead, behind))
        return result

    local[0].wait()
    for n in range(4):
        seg_out[0, n, :B, :B] = dot3(element(lo, n, 1), element(lo, n, 0))
    local[1].wait()
    local[2].wait()
    halo = dot3(prev[...], rst[...], NT)
    for n in range(4):
        hb_first[4 + n, :, :Q] = halo[2 * n : 2 * n + 2]

    @pl.when(odd)
    def _():
        pl.semaphore_wait(barrier, 6)

    @pl.when(jnp.logical_not(odd))
    def _():
        pl.semaphore_wait(barrier, 5)

    def halo_to(i, dp):
        return remote(
            hb_first.at[pl.ds(4, 4)], hb_first.at[pl.ds((1 - dp) * 4, 4)], s_h.at[i], r_h.at[i],
            z_peer(dp),
        )

    def maps_to(i, dp):
        return remote(
            seg_out.at[pl.ds(3, 2)], de.at[1 - dp], s_d.at[i], r_d.at[i], z_peer(dp)
        )

    sides = ((0, 1), (1, -1))
    for side in sides:
        sends.append(lambda side=side: halo_to(*side))
        sends.append(lambda side=side: maps_to(*side))

    @pl.when(jnp.logical_not(odd))
    def _():
        for side in sides:
            halo_to(*side).start()

    maps0 = send_maps(0)
    local[3].wait()
    local[4].wait()
    for n in range(4):
        eb[n, :B, :B] = dot3(element(di, n, 0), element(up, n, 0))
        seg_out[4, n, :B, :B] = dot3(element(di, n, 1), element(up, n, 1))
        seg_out[1, n, :B, :B] = dot3(eb[n, :B, :B], own(4, n))
    maps1 = send_maps(1)
    for n in range(4):
        wb[n, :B, :B] = dot3(eb[n, :B, :B], element(di, n, 1))
        whole = dot3(element(di, n, 0), element(lo, n, 0)) + dot3(wb[n, :B, :B], own(0, n))
        seg_out[2, n, :B, :B] = -whole
    maps2 = send_maps(2)
    for n in range(4):
        seg_out[3, n, :B, :B] = element(di, n, 1)
    for k in (5, 6, 7):
        local[k].wait()

    @pl.when(odd)
    def _():
        for side, other in zip(sides, sides[::-1]):
            halo_to(*side).wait_recv()
            halo_to(*other).start()
        for side in sides:
            maps_to(*side).start()

    @pl.when(jnp.logical_not(odd))
    def _():
        for side in sides:
            maps_to(*side).start()
        for side in sides:
            halo_to(*side).wait_recv()

    first_in = send_local(0, right_sides(0))
    def send_entries(j, d):
        same = remote(
            ent_out.at[j], ent_in.at[y, pl.ds(1, 2)], s_t.at[0, d], r_t.at[0, d], at(0, d)
        )
        beside = remote(
            ent_out.at[j], ent_in.at[y, pl.ds(0, 2)], s_t.at[1, d], r_t.at[0, d], at(1, d)
        )
        below = remote(
            ent_out.at[j, 0], ent_in.at[y, 2], s_t.at[2, d], r_t.at[1, d], at(1, d, -1)
        )
        above = remote(
            ent_out.at[j, 1], ent_in.at[y, 0], s_t.at[3, d], r_t.at[1, d], at(0, d, 1)
        )
        return above, below, same, beside

    def store_entries(ref, done):
        for c in both:
            for j in range(4):
                for row in range(3):
                    ref[j, c, row : row + 1, :B] = done[c][row][j]

    @pl.when(odd)
    def _():
        maps0()
        p01 = [dot3(seg(c, 0, 1), seg(c, 0, 0)) for c in both]
        p23 = [dot3(seg(c, 0, 3), seg(c, 0, 2)) for c in both]
        for c in both:
            part[c, 0, :B, :B] = p01[c]
        quarters0 = send_quarter(0, [dot3(p23[c], p01[c]) for c in both])
        maps1()
        n01 = [dot3(seg(c, 1, 0), seg(c, 1, 1)) for c in both]
        n23 = [dot3(seg(c, 1, 2), seg(c, 1, 3)) for c in both]
        for c in both:
            part[c, 5, :B, :B] = n23[c]
        quarters1 = send_quarter(1, [dot3(n01[c], n23[c]) for c in both])
        maps2()
        k1m0 = [dot3(seg(c, 2, 1), seg(c, 0, 0)) for c in both]
        k01 = [seg(c, 2, 0) + dot3(seg(c, 1, 0), k1m0[c]) for c in both]
        k23 = [
            seg(c, 2, 2) + dot3(seg(c, 1, 2), dot3(seg(c, 2, 3), seg(c, 0, 2))) for c in both
        ]
        quarters2 = send_quarter(
            2, [k01[c] + dot3(n01[c], dot3(k23[c], p01[c])) for c in both]
        )
        first_in()
        starts = quarter_tails(0)
        vectors, ends = send_quarter_vectors(0, starts)
        for c in both:
            p3 = dot3(seg(c, 0, 2), p01[c])
            part[c, 1, :B, :B] = p3
            k2 = dot3(seg(c, 2, 3), p3)
            part[c, 2, :B, :B] = k2
            k1 = dot3(seg(c, 2, 2), p01[c]) + dot3(seg(c, 1, 2), k2)
            part[c, 3, :B, :B] = k1
            part[c, 4, :B, :B] = k1m0[c] + dot3(seg(c, 1, 1), k1)
            part[c, 6, :B, :B] = dot3(seg(c, 1, 1), n23[c])
        quarters0()
        quarters1()
        quarters2()
        vectors()
        done = fields(0, starts, ends)
        store_entries(ent_out, done)
        for d in (2, 1, 3, 0):
            for copy in send_entries(ys[d], d)[: 4 if d else 3]:
                copy.start()
        ent_in[y, pl.ds(0, 2)] = ent_out[y]

    for side in sides:
        maps_to(*side).wait_recv()
    for d in range(4):
        send_entries(0, d)[0].wait_recv()

    for d in (1, 2, 3):
        send_entries(0, d)[3].wait_recv()

    @pl.when(jnp.logical_not(odd))
    def _():
        send_entries(0, 0)[3].wait_recv()

    for o in range(3):
        for n in range(4):
            row = 8 * o + 2 * n
            entry = ent_in[n, o]
            if o == 1:
                pivot, upper = own(3, n), own(4, n)
            else:
                pivot, upper = de[o, 0, n, :B, :B], de[o, 1, n, :B, :B]
            f24[row : row + 1, :] = entry[0:1, :B]
            f24[row + 1 : row + 2, :] = apply2(pivot, entry[1:2, :B], upper, -entry[2:3, :B])
    halo = dot3(f24[...], rst[...], NT)
    for m in range(12):
        hb_second[m, :, :Q] = halo[2 * m : 2 * m + 2]
    second_in = send_local(1, right_sides(1))

    def send_field(d):
        even = remote(fx.at[ys[d], 0], ob.at[y], s_f.at[0, d], r_f.at[d], at(0, d))
        beside = remote(fx.at[ys[d], 1], ob.at[y], s_f.at[1, d], r_f.at[d], at(1, d))
        return even, beside

    @pl.when(odd)
    def _():
        second_in()
        starts = quarter_tails(1)
        vectors, ends = send_quarter_vectors(1, starts)
        vectors()
        done = fields(1, starts, ends)
        store_entries(fx, done)
        for d in (2, 1, 3, 0):
            for copy in send_field(d)[: 2 if d else 1]:
                copy.start()
        ob[y] = fx[y, 1]

    for d in (1, 2, 3):
        send_field(d)[0].wait_recv()

    @pl.when(jnp.logical_not(odd))
    def _():
        send_field(0)[0].wait_recv()

    for n in range(4):
        entry = ob[n]
        out[2 * n : 2 * n + 1, :] = entry[0:1, :B]
        out[2 * n + 1 : 2 * n + 2, :] = apply2(
            own(3, n), entry[1:2, :B], own(4, n), -entry[2:3, :B]
        )
    for make in sends:
        make().wait_send()

    @pl.when(jnp.logical_not(odd))
    def _():
        for make in sends_even:
            make().wait_send()

    @pl.when(odd)
    def _():
        for make in sends_odd:
            make().wait_send()
        for d in range(4):
            for copy in send_entries(0, d)[: 4 if d else 3]:
                copy.wait_send()
            for copy in send_field(d)[: 2 if d else 1]:
                copy.wait_send()


def per_device(residual, previous, lower, pivot, upper, couple, restrict, neighbours):
    def factor(a):
        return jnp.transpose(a, (0, 2, 1, 3)).reshape(4, 2 * B, B)

    dma = pltpu.SemaphoreType.DMA
    result = pl.pallas_call(
        kernel,
        out_shape=jax.ShapeDtypeStruct((8, B), F32),
        in_specs=[pl.BlockSpec(memory_space=pl.ANY)] * 8,
        out_specs=pl.BlockSpec(memory_space=pltpu.VMEM),
        scratch_shapes=[
            pltpu.SMEM((4, 4), jnp.int32),
            pltpu.VMEM((8, B), F32),
            pltpu.VMEM((8, B), F32),
            pltpu.VMEM((Q, B), F32),
            pltpu.VMEM((4, 2 * B, B), F32),
            pltpu.VMEM((4, 2 * B, B), F32),
            pltpu.VMEM((4, 2 * B, B), F32),
            pltpu.VMEM((4, 2, Q, B), F32),
            pltpu.VMEM((4, 104, 128), F32),
            pltpu.VMEM((4, 104, 128), F32),
            pltpu.VMEM((5, 4, 104, 128), F32),
            pltpu.VMEM((2, 3, 4, 104, 128), F32),
            pltpu.VMEM((4, 3, 2, 104, 128), F32),
            pltpu.VMEM((2, 7, 104, 128), F32),
            pltpu.VMEM((3, 2, 4, 104, 128), F32),
            pltpu.VMEM((12, 2, 256), F32),
            pltpu.VMEM((12, 2, 256), F32),
            pltpu.VMEM((8, Q), F32),
            pltpu.VMEM((24, B), F32),
            pltpu.VMEM((4, 2, 4, 128), F32),
            pltpu.VMEM((4, 3, 4, 128), F32),
            pltpu.VMEM((2, 4, 2, 128), F32),
            pltpu.VMEM((2, 2, 4, 2, 128), F32),
            pltpu.VMEM((2, 4, 2, 2, 128), F32),
            pltpu.VMEM((4, 2, 4, 128), F32),
            pltpu.VMEM((4, 4, 128), F32),
            dma((8,)),
            dma((2,)),
            dma((2,)),
            dma((3, 4)),
            dma((2, 3, 4)),
            dma((3, 4)),
            dma((3, 4)),
            dma((2,)),
            dma((2,)),
            dma((2, 4)),
            dma((2, 2, 4)),
            dma((2, 4)),
            dma((2, 4)),
            dma((4, 4)),
            dma((2, 4)),
            dma((2, 4)),
            dma((4,)),
        ],
        compiler_params=pltpu.CompilerParams(
            collective_id=0, has_side_effects=True, vmem_limit_bytes=60 << 20
        ),
    )(
        neighbours,
        residual.reshape(8, B),
        previous.reshape(8, B),
        jnp.transpose(restrict, (1, 0, 2)).reshape(Q, B),
        factor(lower),
        factor(pivot),
        factor(upper),
        jnp.transpose(couple, (0, 1, 4, 2, 3)).reshape(4, 2, Q, B),
    )
    return result.reshape(4, 2, B)


def solution(mesh):
    placed = (
        P("patch", "line", None),
        P("patch", "line", None),
        P("patch", "line", None, None),
        P("patch", "line", None, None),
        P("patch", "line", None, None),
        P("patch", "line", None, None, None),
        P(),
        P("patch", None),
    )
    return jax.shard_map(
        per_device, mesh=mesh, in_specs=placed, out_specs=P("patch", "line", None), check_vma=False
    )
```

```python
import jax
import jax.numpy as jnp
from jax import lax
from jax.experimental import pallas as pl
from jax.experimental.pallas import tpu as pltpu
from jax.sharding import PartitionSpec as P

F32 = jnp.float32
BF16 = jnp.bfloat16
MESH = pl.DeviceIdType.MESH
B = 100
Q = 200
NP = 32
NN = (((1,), (0,)), ((), ()))
NT = (((1,), (1,)), ((), ()))


def split(a):
    high = a.astype(BF16)
    return high, (a - high.astype(F32)).astype(BF16)


def dot3(a, b, dims=NN):
    ah, al = split(a)
    bh, bl = split(b)

    def mm(u, v):
        return lax.dot_general(u, v, dims, preferred_element_type=F32)

    return mm(ah, bh) + (mm(ah, bl) + mm(al, bh))


def kernel(
    nb_any, res_any, prev_any, rst_any, low, piv, upp, fc, out,
    nb, res, prev, rst, lo, di, up, fo, wfc,
    eb, wb, seg_out, seg_in, quarter, part, de, hb_first, hb_second, lhs, f24, ent_out, ent_in,
    a_out, a_in, th, fx, ob,
    s_loc, s_d, r_d, s_m, r_m, s_q, r_q, s_h, r_h, s_a, r_a, s_x, r_x, s_t, r_t, s_f, r_f,
):
    p = lax.axis_index("patch")
    line = lax.axis_index("line")
    x, y = line // 4, line % 4
    z, core = p // 2, p % 2
    ys = [(y + d) % 4 for d in range(4)]
    odd = core == 1

    def at(c, d, dz=0):
        return (((z + dz + NP // 2) % (NP // 2)) * 2 + c, x * 4 + ys[d])

    def x_peer(d):
        return (p, ((x + d) % 4) * 4 + y)

    def z_peer(d):
        return ((p + d + NP) % NP, line)

    def remote(src, dst, send, recv, device):
        return pltpu.make_async_remote_copy(
            src_ref=src, dst_ref=dst, send_sem=send, recv_sem=recv,
            device_id=device, device_id_type=MESH,
        )

    barrier = pltpu.get_barrier_semaphore()

    def greet(device):
        pl.semaphore_signal(barrier, inc=1, device_id=device, device_id_type=MESH)

    @pl.when(odd)
    def _():
        for d in (2, 1, 3):
            greet(at(1, d))
            greet(x_peer(d))
        greet(at(0, 0, 1))
        for d in (2, 1, 3, 0):
            greet(at(0, d))

    pairs = (
        (low, lo), (prev_any, prev), (rst_any, rst), (piv, di), (upp, up),
        (nb_any, nb), (res_any, res), (fc, fo),
    )
    local = [
        pltpu.make_async_copy(src, dst, s_loc.at[k]) for k, (src, dst) in enumerate(pairs)
    ]
    for copy in local:
        copy.start()

    hb = (hb_first, hb_second)
    sends = []
    sends_even = []
    sends_odd = []
    eye = lax.broadcasted_iota(jnp.int32, (B, B), 0) == lax.broadcasted_iota(
        jnp.int32, (B, B), 1
    )

    def to_row(column):
        return jnp.sum(jnp.where(eye, column, 0.0), axis=0, keepdims=True)

    def apply(matrix, row):
        return to_row(jnp.sum(matrix * row, axis=1, keepdims=True))

    def apply2(one, u, two, v):
        return to_row(jnp.sum(one * u + two * v, axis=1, keepdims=True))

    def element(ref, n, l):
        return ref[n, pl.ds(l, B, stride=2), :]

    def own(k, n):
        return seg_out[k, n, :B, :B]

    def to_owner(src, dst, send, recv):
        def make(d):
            return remote(src(ys[d]), dst(core, y), send.at[d], recv(core, d), at(1, d))

        for d in (2, 1, 3):
            make(d).start()
            sends.append(lambda d=d: make(d))

        @pl.when(jnp.logical_not(odd))
        def _():
            make(0).start()

        sends_even.append(lambda: make(0))

        @pl.when(odd)
        def _():
            dst(1, y)[...] = src(y)[...]

        def wait(d, c):
            remote(src(0), dst(c, 0), send.at[d], recv(c, d), at(1, 1)).wait_recv()

        def arrived():
            for d in (0, 1, 3, 2):
                wait(d, 0)
            for d in (1, 3, 2):
                wait(d, 1)

        return arrived

    def send_maps(k):
        return to_owner(
            lambda n: seg_out.at[k, n], lambda c, j: seg_in.at[c, k, j], s_m.at[k],
            lambda c, d: r_m.at[c, k, d],
        )

    lane = lax.broadcasted_iota(jnp.int32, (2, Q), 1) % 4

    def pick(block, source, f):
        total = jnp.zeros(block.shape, F32)
        for g in range(4):
            moved = block if g == f else pltpu.roll(block, (f - g) % 256, axis=1)
            total = jnp.where(source == g, moved, total)
        return jnp.where(lane == f, total[:, :Q], 0.0)

    def right_sides(sweep):
        for n in range(4):
            picked = jnp.zeros((2, Q), F32)
            for f in range(4):
                entry = nb[n, f]
                picked = picked + pick(
                    hb[sweep][entry // 4], entry % 4, f
                )
            lhs[2 * n : 2 * n + 2, :Q] = picked
        whole = lhs[...]
        high = whole.astype(BF16).astype(F32)
        halves = jnp.concatenate([high, whole - high], axis=0).astype(BF16)
        rows = []
        for row in range(8):
            got = lax.dot_general(halves, wfc[row], NN, preferred_element_type=F32)
            low = got[row : row + 1, 128 : 128 + B] + got[row + 8 : row + 9, :B]
            rows.append(res[row : row + 1, :] - (got[row : row + 1, :B] + low))
        return rows

    def send_local(sweep, rows):
        tails = []
        for n in range(4):
            tails.append(rows[2 * n + 1] - apply(element(lo, n, 1), rows[2 * n]))
        for n in range(4):
            a_out[sweep, n, 0:1, :B] = tails[n]
            a_out[sweep, n, 1:2, :B] = apply2(
                element(di, n, 0), rows[2 * n], wb[n, :B, :B], -tails[n]
            )
        return to_owner(
            lambda n: a_out.at[sweep, n], lambda c, j: a_in.at[sweep, c, j], s_a.at[sweep],
            lambda c, d: r_a.at[sweep, c, d],
        )

    both = (0, 1)

    def seg(c, k, j):
        return seg_in[c, k, j, :B, :B]

    def q(c, j, k):
        return quarter[j, k, c, :B, :B]

    def across(make):
        for d in (2, 1, 3):
            make(d).start()
            sends_odd.append(lambda d=d: make(d))

        def arrived():
            for d in (1, 3, 2):
                make(d).wait_recv()

        return arrived

    def send_quarter(k, values):
        for c in both:
            quarter[x, k, c, :B, :B] = values[c]
        return across(
            lambda d: remote(
                quarter.at[x, k], quarter.at[x, k], s_q.at[k, d], r_q.at[k, d], x_peer(d)
            )
        )

    def quarter_tails(sweep):
        tails = [[a_in[sweep, c, j, 0:1, :B] for j in range(4)] for c in both]
        y2 = [tails[c][1] + apply(seg(c, 0, 1), tails[c][0]) for c in both]
        y3 = [tails[c][2] + apply(seg(c, 0, 2), y2[c]) for c in both]
        last = [tails[c][3] + apply(seg(c, 0, 3), y3[c]) for c in both]
        return [(None, tails[c][0], y2[c], y3[c], last[c]) for c in both]

    def send_quarter_vectors(sweep, starts):
        heads = [[a_in[sweep, c, j, 1:2, :B] for j in range(4)] for c in both]
        ends = [[None, None, None, h[3]] for h in heads]
        g3 = [heads[c][3] + apply(seg(c, 2, 3), starts[c][3]) for c in both]
        g2 = [
            heads[c][2] + apply2(seg(c, 2, 2), starts[c][2], seg(c, 1, 2), g3[c]) for c in both
        ]
        g1 = [
            heads[c][1] + apply2(seg(c, 2, 1), starts[c][1], seg(c, 1, 1), g2[c]) for c in both
        ]
        g0 = [heads[c][0] + apply(seg(c, 1, 0), g1[c]) for c in both]
        for c in both:
            th[sweep, x, c, 0:1, :B] = starts[c][4]
            th[sweep, x, c, 1:2, :B] = g0[c]
        arrived = across(
            lambda d: remote(
                th.at[sweep, x], th.at[sweep, x], s_x.at[sweep, d], r_x.at[sweep, d], x_peer(d)
            )
        )
        return arrived, [(g0[c], g1[c], g2[c], g3[c]) for c in both]

    def mine(values):
        total = values[0]
        for j in range(1, 4):
            total = jnp.where(x == j, values[j], total)
        return total

    def fields(sweep, starts, ends):
        tail = [[th[sweep, j, c, 0:1, :B] for j in range(4)] for c in both]
        head = [[th[sweep, j, c, 1:2, :B] for j in range(4)] for c in both]
        zero = jnp.zeros((1, B), F32)
        y2 = [tail[c][1] + apply(q(c, 1, 0), tail[c][0]) for c in both]
        y3 = [tail[c][2] + apply(q(c, 2, 0), y2[c]) for c in both]
        h3 = [head[c][3] + apply(q(c, 3, 2), y3[c]) for c in both]
        h2 = [head[c][2] + apply2(q(c, 2, 2), y2[c], q(c, 2, 1), h3[c]) for c in both]
        h1 = [head[c][1] + apply2(q(c, 1, 2), tail[c][0], q(c, 1, 1), h2[c]) for c in both]
        result = []
        for c in both:
            y_in = mine((zero, tail[c][0], y2[c], y3[c]))
            x_in = mine((h1[c], h2[c], h3[c], zero))
            ahead = [
                starts[c][1] + apply(seg(c, 0, 0), y_in),
                starts[c][2] + apply(part[c, 0, :B, :B], y_in),
                starts[c][3] + apply(part[c, 1, :B, :B], y_in),
                starts[c][4] + apply(quarter[x, 0, c, :B, :B], y_in),
            ]
            g0, g1, g2, g3 = ends[c]
            first = [
                g0 + apply2(quarter[x, 2, c, :B, :B], y_in, quarter[x, 1, c, :B, :B], x_in),
                g1 + apply2(part[c, 4, :B, :B], y_in, part[c, 6, :B, :B], x_in),
                g2 + apply2(part[c, 3, :B, :B], y_in, part[c, 5, :B, :B], x_in),
                g3 + apply2(part[c, 2, :B, :B], y_in, seg(c, 1, 3), x_in),
            ]
            behind = first[1:] + [x_in]
            result.append((first, ahead, behind))
        return result

    local[0].wait()
    for n in range(4):
        seg_out[0, n, :B, :B] = dot3(element(lo, n, 1), element(lo, n, 0))
    local[1].wait()
    local[2].wait()
    halo = dot3(prev[...], rst[...], NT)
    for n in range(4):
        hb_first[4 + n, :, :Q] = halo[2 * n : 2 * n + 2]

    @pl.when(odd)
    def _():
        pl.semaphore_wait(barrier, 6)

    @pl.when(jnp.logical_not(odd))
    def _():
        pl.semaphore_wait(barrier, 5)

    def halo_to(i, dp):
        return remote(
            hb_first.at[pl.ds(4, 4)], hb_first.at[pl.ds((1 - dp) * 4, 4)], s_h.at[i], r_h.at[i],
            z_peer(dp),
        )

    def maps_to(i, dp):
        return remote(
            seg_out.at[pl.ds(3, 2)], de.at[1 - dp], s_d.at[i], r_d.at[i], z_peer(dp)
        )

    sides = ((0, 1), (1, -1))
    for side in sides:
        sends.append(lambda side=side: halo_to(*side))
        sends.append(lambda side=side: maps_to(*side))

    @pl.when(jnp.logical_not(odd))
    def _():
        for side in sides:
            halo_to(*side).start()

    maps0 = send_maps(0)
    local[3].wait()
    local[4].wait()
    for n in range(4):
        eb[n, :B, :B] = dot3(element(di, n, 0), element(up, n, 0))
        seg_out[4, n, :B, :B] = dot3(element(di, n, 1), element(up, n, 1))
        seg_out[1, n, :B, :B] = dot3(eb[n, :B, :B], own(4, n))
    maps1 = send_maps(1)
    for n in range(4):
        wb[n, :B, :B] = dot3(eb[n, :B, :B], element(di, n, 1))
        whole = dot3(element(di, n, 0), element(lo, n, 0)) + dot3(wb[n, :B, :B], own(0, n))
        seg_out[2, n, :B, :B] = -whole
    maps2 = send_maps(2)
    for n in range(4):
        seg_out[3, n, :B, :B] = element(di, n, 1)

    @pl.when(odd)
    def _():
        for side, other in zip(sides, sides[::-1]):
            halo_to(*side).wait_recv()
            halo_to(*other).start()
        for side in sides:
            maps_to(*side).start()

    @pl.when(jnp.logical_not(odd))
    def _():
        for side in sides:
            maps_to(*side).start()

    for k in (5, 6, 7):
        local[k].wait()
    lhs[:, Q:] = jnp.zeros((8, 8), F32)
    for row in range(8):
        high, rest = split(
            jnp.concatenate([fo[row // 2, row % 2], jnp.zeros((8, B), F32)], axis=0)
        )
        wfc[row, :, :B] = high
        wfc[row, :, 128 : 128 + B] = rest

    @pl.when(jnp.logical_not(odd))
    def _():
        for side in sides:
            halo_to(*side).wait_recv()

    first_in = send_local(0, right_sides(0))
    def send_entries(j, d):
        same = remote(
            ent_out.at[j], ent_in.at[y, pl.ds(1, 2)], s_t.at[0, d], r_t.at[0, d], at(0, d)
        )
        beside = remote(
            ent_out.at[j], ent_in.at[y, pl.ds(0, 2)], s_t.at[1, d], r_t.at[0, d], at(1, d)
        )
        below = remote(
            ent_out.at[j, 0], ent_in.at[y, 2], s_t.at[2, d], r_t.at[1, d], at(1, d, -1)
        )
        above = remote(
            ent_out.at[j, 1], ent_in.at[y, 0], s_t.at[3, d], r_t.at[1, d], at(0, d, 1)
        )
        return above, below, same, beside

    def store_entries(ref, done):
        for c in both:
            for j in range(4):
                for row in range(3):
                    ref[j, c, row : row + 1, :B] = done[c][row][j]

    @pl.when(odd)
    def _():
        maps0()
        p01 = [dot3(seg(c, 0, 1), seg(c, 0, 0)) for c in both]
        p23 = [dot3(seg(c, 0, 3), seg(c, 0, 2)) for c in both]
        for c in both:
            part[c, 0, :B, :B] = p01[c]
        quarters0 = send_quarter(0, [dot3(p23[c], p01[c]) for c in both])
        maps1()
        n01 = [dot3(seg(c, 1, 0), seg(c, 1, 1)) for c in both]
        n23 = [dot3(seg(c, 1, 2), seg(c, 1, 3)) for c in both]
        for c in both:
            part[c, 5, :B, :B] = n23[c]
        quarters1 = send_quarter(1, [dot3(n01[c], n23[c]) for c in both])
        maps2()
        k1m0 = [dot3(seg(c, 2, 1), seg(c, 0, 0)) for c in both]
        k01 = [seg(c, 2, 0) + dot3(seg(c, 1, 0), k1m0[c]) for c in both]
        k23 = [
            seg(c, 2, 2) + dot3(seg(c, 1, 2), dot3(seg(c, 2, 3), seg(c, 0, 2))) for c in both
        ]
        quarters2 = send_quarter(
            2, [k01[c] + dot3(n01[c], dot3(k23[c], p01[c])) for c in both]
        )
        first_in()
        starts = quarter_tails(0)
        vectors, ends = send_quarter_vectors(0, starts)
        for c in both:
            p3 = dot3(seg(c, 0, 2), p01[c])
            part[c, 1, :B, :B] = p3
            k2 = dot3(seg(c, 2, 3), p3)
            part[c, 2, :B, :B] = k2
            k1 = dot3(seg(c, 2, 2), p01[c]) + dot3(seg(c, 1, 2), k2)
            part[c, 3, :B, :B] = k1
            part[c, 4, :B, :B] = k1m0[c] + dot3(seg(c, 1, 1), k1)
            part[c, 6, :B, :B] = dot3(seg(c, 1, 1), n23[c])
        quarters0()
        quarters1()
        quarters2()
        vectors()
        done = fields(0, starts, ends)
        store_entries(ent_out, done)
        for d in (2, 1, 3, 0):
            for copy in send_entries(ys[d], d)[: 4 if d else 3]:
                copy.start()
        ent_in[y, pl.ds(0, 2)] = ent_out[y]

    for side in sides:
        maps_to(*side).wait_recv()
    for d in range(4):
        send_entries(0, d)[0].wait_recv()

    for d in (1, 2, 3):
        send_entries(0, d)[3].wait_recv()

    @pl.when(jnp.logical_not(odd))
    def _():
        send_entries(0, 0)[3].wait_recv()

    for o in range(3):
        for n in range(4):
            row = 8 * o + 2 * n
            entry = ent_in[n, o]
            if o == 1:
                pivot, upper = own(3, n), own(4, n)
            else:
                pivot, upper = de[o, 0, n, :B, :B], de[o, 1, n, :B, :B]
            f24[row : row + 1, :] = entry[0:1, :B]
            f24[row + 1 : row + 2, :] = apply2(pivot, entry[1:2, :B], upper, -entry[2:3, :B])
    halo = dot3(f24[...], rst[...], NT)
    for m in range(12):
        hb_second[m, :, :Q] = halo[2 * m : 2 * m + 2]
    second_in = send_local(1, right_sides(1))

    def send_field(d):
        even = remote(fx.at[ys[d], 0], ob.at[y], s_f.at[0, d], r_f.at[d], at(0, d))
        beside = remote(fx.at[ys[d], 1], ob.at[y], s_f.at[1, d], r_f.at[d], at(1, d))
        return even, beside

    @pl.when(odd)
    def _():
        second_in()
        starts = quarter_tails(1)
        vectors, ends = send_quarter_vectors(1, starts)
        vectors()
        done = fields(1, starts, ends)
        store_entries(fx, done)
        for d in (2, 1, 3, 0):
            for copy in send_field(d)[: 2 if d else 1]:
                copy.start()
        ob[y] = fx[y, 1]

    for d in (1, 2, 3):
        send_field(d)[0].wait_recv()

    @pl.when(jnp.logical_not(odd))
    def _():
        send_field(0)[0].wait_recv()

    for n in range(4):
        entry = ob[n]
        out[2 * n : 2 * n + 1, :] = entry[0:1, :B]
        out[2 * n + 1 : 2 * n + 2, :] = apply2(
            own(3, n), entry[1:2, :B], own(4, n), -entry[2:3, :B]
        )
    for make in sends:
        make().wait_send()

    @pl.when(jnp.logical_not(odd))
    def _():
        for make in sends_even:
            make().wait_send()

    @pl.when(odd)
    def _():
        for make in sends_odd:
            make().wait_send()
        for d in range(4):
            for copy in send_entries(0, d)[: 4 if d else 3]:
                copy.wait_send()
            for copy in send_field(d)[: 2 if d else 1]:
                copy.wait_send()


def per_device(residual, previous, lower, pivot, upper, couple, restrict, neighbours):
    def factor(a):
        return jnp.transpose(a, (0, 2, 1, 3)).reshape(4, 2 * B, B)

    dma = pltpu.SemaphoreType.DMA
    result = pl.pallas_call(
        kernel,
        out_shape=jax.ShapeDtypeStruct((8, B), F32),
        in_specs=[pl.BlockSpec(memory_space=pl.ANY)] * 8,
        out_specs=pl.BlockSpec(memory_space=pltpu.VMEM),
        scratch_shapes=[
            pltpu.SMEM((4, 4), jnp.int32),
            pltpu.VMEM((8, B), F32),
            pltpu.VMEM((8, B), F32),
            pltpu.VMEM((Q, B), F32),
            pltpu.VMEM((4, 2 * B, B), F32),
            pltpu.VMEM((4, 2 * B, B), F32),
            pltpu.VMEM((4, 2 * B, B), F32),
            pltpu.VMEM((4, 2, Q, B), F32),
            pltpu.VMEM((8, Q + 8, 256), BF16),
            pltpu.VMEM((4, 104, 128), F32),
            pltpu.VMEM((4, 104, 128), F32),
            pltpu.VMEM((5, 4, 104, 128), F32),
            pltpu.VMEM((2, 3, 4, 104, 128), F32),
            pltpu.VMEM((4, 3, 2, 104, 128), F32),
            pltpu.VMEM((2, 7, 104, 128), F32),
            pltpu.VMEM((3, 2, 4, 104, 128), F32),
            pltpu.VMEM((12, 2, 256), F32),
            pltpu.VMEM((12, 2, 256), F32),
            pltpu.VMEM((8, Q + 8), F32),
            pltpu.VMEM((24, B), F32),
            pltpu.VMEM((4, 2, 4, 128), F32),
            pltpu.VMEM((4, 3, 4, 128), F32),
            pltpu.VMEM((2, 4, 2, 128), F32),
            pltpu.VMEM((2, 2, 4, 2, 128), F32),
            pltpu.VMEM((2, 4, 2, 2, 128), F32),
            pltpu.VMEM((4, 2, 4, 128), F32),
            pltpu.VMEM((4, 4, 128), F32),
            dma((8,)),
            dma((2,)),
            dma((2,)),
            dma((3, 4)),
            dma((2, 3, 4)),
            dma((3, 4)),
            dma((3, 4)),
            dma((2,)),
            dma((2,)),
            dma((2, 4)),
            dma((2, 2, 4)),
            dma((2, 4)),
            dma((2, 4)),
            dma((4, 4)),
            dma((2, 4)),
            dma((2, 4)),
            dma((4,)),
        ],
        compiler_params=pltpu.CompilerParams(
            collective_id=0, has_side_effects=True, vmem_limit_bytes=60 << 20
        ),
    )(
        neighbours,
        residual.reshape(8, B),
        previous.reshape(8, B),
        jnp.transpose(restrict, (1, 0, 2)).reshape(Q, B),
        factor(lower),
        factor(pivot),
        factor(upper),
        jnp.transpose(couple, (0, 1, 4, 2, 3)).reshape(4, 2, Q, B),
    )
    return result.reshape(4, 2, B)


def solution(mesh):
    placed = (
        P("patch", "line", None),
        P("patch", "line", None),
        P("patch", "line", None, None),
        P("patch", "line", None, None),
        P("patch", "line", None, None),
        P("patch", "line", None, None, None),
        P(),
        P("patch", None),
    )
    return jax.shard_map(
        per_device, mesh=mesh, in_specs=placed, out_specs=P("patch", "line", None), check_vma=False
    )
```

```python
import jax
import jax.numpy as jnp
from jax import lax
from jax.experimental import pallas as pl
from jax.experimental.pallas import tpu as pltpu
from jax.sharding import PartitionSpec as P

F32 = jnp.float32
BF16 = jnp.bfloat16
MESH = pl.DeviceIdType.MESH
B = 100
Q = 200
NP = 32
NN = (((1,), (0,)), ((), ()))
NT = (((1,), (1,)), ((), ()))


def split(a):
    high = a.astype(BF16)
    return high, (a - high.astype(F32)).astype(BF16)


def dot3(a, b, dims=NN):
    ah, al = split(a)
    bh, bl = split(b)

    def mm(u, v):
        return lax.dot_general(u, v, dims, preferred_element_type=F32)

    return mm(ah, bh) + (mm(ah, bl) + mm(al, bh))


def kernel(
    nb_any, res_any, prev_any, rst_any, low, piv, upp, fc, out,
    nb, res, prev, rst, lo, di, up, fo, wfc,
    eb, wb, seg_out, seg_in, quarter, part, de, hb_first, hb_second, lhs, f24, ent_out, ent_in,
    a_out, a_in, th, fx, ob,
    s_loc, s_d, r_d, s_m, r_m, s_q, r_q, s_h, r_h, s_a, r_a, s_x, r_x, s_t, r_t, s_f, r_f,
):
    p = lax.axis_index("patch")
    line = lax.axis_index("line")
    x, y = line // 4, line % 4
    ys = [(y + d) % 4 for d in range(4)]

    def at(d, dp=0):
        return ((p + dp + NP) % NP, x * 4 + ys[d])

    def x_peer(d):
        return (p, ((x + d) % 4) * 4 + y)

    def z_peer(d):
        return ((p + d + NP) % NP, line)

    def remote(src, dst, send, recv, device):
        return pltpu.make_async_remote_copy(
            src_ref=src, dst_ref=dst, send_sem=send, recv_sem=recv,
            device_id=device, device_id_type=MESH,
        )

    barrier = pltpu.get_barrier_semaphore()

    def greet(device):
        pl.semaphore_signal(barrier, inc=1, device_id=device, device_id_type=MESH)

    for d in (2, 1, 3):
        greet(at(d))
        greet(x_peer(d))
    greet(at(0, 1))
    greet(at(0, -1))
    pairs = (
        (low, lo), (prev_any, prev), (rst_any, rst), (piv, di), (upp, up),
        (nb_any, nb), (res_any, res), (fc, fo),
    )
    local = [
        pltpu.make_async_copy(src, dst, s_loc.at[k]) for k, (src, dst) in enumerate(pairs)
    ]
    for copy in local:
        copy.start()

    hb = (hb_first, hb_second)
    sends = []
    eye = lax.broadcasted_iota(jnp.int32, (B, B), 0) == lax.broadcasted_iota(
        jnp.int32, (B, B), 1
    )

    def to_row(column):
        return jnp.sum(jnp.where(eye, column, 0.0), axis=0, keepdims=True)

    def apply(matrix, row):
        return to_row(jnp.sum(matrix * row, axis=1, keepdims=True))

    def apply2(one, u, two, v):
        return to_row(jnp.sum(one * u + two * v, axis=1, keepdims=True))

    def element(ref, n, l):
        return ref[n, pl.ds(l, B, stride=2), :]

    def own(k, n):
        return seg_out[k, n, :B, :B]

    def to_owner(src, dst, send, recv):
        def make(d):
            return remote(src(ys[d]), dst(0, y), send.at[d], recv(0, d), at(d))

        for d in (2, 1, 3):
            make(d).start()
            sends.append(lambda d=d: make(d))
        dst(0, y)[...] = src(y)[...]

        def arrived():
            for d in (1, 3, 2):
                make(d).wait_recv()

        return arrived

    def send_maps(k):
        return to_owner(
            lambda n: seg_out.at[k, n], lambda c, j: seg_in.at[c, k, j], s_m.at[k],
            lambda c, d: r_m.at[c, k, d],
        )

    lane = lax.broadcasted_iota(jnp.int32, (2, Q), 1) % 4

    def pick(block, source, f):
        total = jnp.zeros(block.shape, F32)
        for g in range(4):
            moved = block if g == f else pltpu.roll(block, (f - g) % 256, axis=1)
            total = jnp.where(source == g, moved, total)
        return jnp.where(lane == f, total[:, :Q], 0.0)

    def right_sides(sweep):
        for n in range(4):
            picked = jnp.zeros((2, Q), F32)
            for f in range(4):
                entry = nb[n, f]
                picked = picked + pick(
                    hb[sweep][entry // 4], entry % 4, f
                )
            lhs[2 * n : 2 * n + 2, :Q] = picked
        whole = lhs[...]
        high = whole.astype(BF16).astype(F32)
        halves = jnp.concatenate([high, whole - high], axis=0).astype(BF16)
        rows = []
        for row in range(8):
            got = lax.dot_general(halves, wfc[row], NN, preferred_element_type=F32)
            low = got[row : row + 1, 128 : 128 + B] + got[row + 8 : row + 9, :B]
            rows.append(res[row : row + 1, :] - (got[row : row + 1, :B] + low))
        return rows

    def send_local(sweep, rows):
        tails = []
        for n in range(4):
            tails.append(rows[2 * n + 1] - apply(element(lo, n, 1), rows[2 * n]))
        for n in range(4):
            a_out[sweep, n, 0:1, :B] = tails[n]
            a_out[sweep, n, 1:2, :B] = apply2(
                element(di, n, 0), rows[2 * n], wb[n, :B, :B], -tails[n]
            )
        return to_owner(
            lambda n: a_out.at[sweep, n], lambda c, j: a_in.at[sweep, c, j], s_a.at[sweep],
            lambda c, d: r_a.at[sweep, c, d],
        )

    both = (0,)

    def seg(c, k, j):
        return seg_in[c, k, j, :B, :B]

    def q(c, j, k):
        return quarter[j, k, c, :B, :B]

    def across(make):
        for d in (2, 1, 3):
            make(d).start()
            sends.append(lambda d=d: make(d))

        def arrived():
            for d in (1, 3, 2):
                make(d).wait_recv()

        return arrived

    def send_quarter(k, values):
        for c in both:
            quarter[x, k, c, :B, :B] = values[c]
        return across(
            lambda d: remote(
                quarter.at[x, k], quarter.at[x, k], s_q.at[k, d], r_q.at[k, d], x_peer(d)
            )
        )

    def quarter_tails(sweep):
        tails = [[a_in[sweep, c, j, 0:1, :B] for j in range(4)] for c in both]
        y2 = [tails[c][1] + apply(seg(c, 0, 1), tails[c][0]) for c in both]
        y3 = [tails[c][2] + apply(seg(c, 0, 2), y2[c]) for c in both]
        last = [tails[c][3] + apply(seg(c, 0, 3), y3[c]) for c in both]
        return [(None, tails[c][0], y2[c], y3[c], last[c]) for c in both]

    def send_quarter_vectors(sweep, starts):
        heads = [[a_in[sweep, c, j, 1:2, :B] for j in range(4)] for c in both]
        ends = [[None, None, None, h[3]] for h in heads]
        g3 = [heads[c][3] + apply(seg(c, 2, 3), starts[c][3]) for c in both]
        g2 = [
            heads[c][2] + apply2(seg(c, 2, 2), starts[c][2], seg(c, 1, 2), g3[c]) for c in both
        ]
        g1 = [
            heads[c][1] + apply2(seg(c, 2, 1), starts[c][1], seg(c, 1, 1), g2[c]) for c in both
        ]
        g0 = [heads[c][0] + apply(seg(c, 1, 0), g1[c]) for c in both]
        for c in both:
            th[sweep, x, c, 0:1, :B] = starts[c][4]
            th[sweep, x, c, 1:2, :B] = g0[c]
        arrived = across(
            lambda d: remote(
                th.at[sweep, x], th.at[sweep, x], s_x.at[sweep, d], r_x.at[sweep, d], x_peer(d)
            )
        )
        return arrived, [(g0[c], g1[c], g2[c], g3[c]) for c in both]

    def mine(values):
        total = values[0]
        for j in range(1, 4):
            total = jnp.where(x == j, values[j], total)
        return total

    def fields(sweep, starts, ends):
        tail = [[th[sweep, j, c, 0:1, :B] for j in range(4)] for c in both]
        head = [[th[sweep, j, c, 1:2, :B] for j in range(4)] for c in both]
        zero = jnp.zeros((1, B), F32)
        y2 = [tail[c][1] + apply(q(c, 1, 0), tail[c][0]) for c in both]
        y3 = [tail[c][2] + apply(q(c, 2, 0), y2[c]) for c in both]
        h3 = [head[c][3] + apply(q(c, 3, 2), y3[c]) for c in both]
        h2 = [head[c][2] + apply2(q(c, 2, 2), y2[c], q(c, 2, 1), h3[c]) for c in both]
        h1 = [head[c][1] + apply2(q(c, 1, 2), tail[c][0], q(c, 1, 1), h2[c]) for c in both]
        result = []
        for c in both:
            y_in = mine((zero, tail[c][0], y2[c], y3[c]))
            x_in = mine((h1[c], h2[c], h3[c], zero))
            ahead = [
                starts[c][1] + apply(seg(c, 0, 0), y_in),
                starts[c][2] + apply(part[c, 0, :B, :B], y_in),
                starts[c][3] + apply(part[c, 1, :B, :B], y_in),
                starts[c][4] + apply(quarter[x, 0, c, :B, :B], y_in),
            ]
            g0, g1, g2, g3 = ends[c]
            first = [
                g0 + apply2(quarter[x, 2, c, :B, :B], y_in, quarter[x, 1, c, :B, :B], x_in),
                g1 + apply2(part[c, 4, :B, :B], y_in, part[c, 6, :B, :B], x_in),
                g2 + apply2(part[c, 3, :B, :B], y_in, part[c, 5, :B, :B], x_in),
                g3 + apply2(part[c, 2, :B, :B], y_in, seg(c, 1, 3), x_in),
            ]
            behind = first[1:] + [x_in]
            result.append((first, ahead, behind))
        return result

    local[0].wait()
    for n in range(4):
        seg_out[0, n, :B, :B] = dot3(element(lo, n, 1), element(lo, n, 0))
    local[1].wait()
    local[2].wait()
    halo = dot3(prev[...], rst[...], NT)
    for n in range(4):
        hb_first[4 + n, :, :Q] = halo[2 * n : 2 * n + 2]

    pl.semaphore_wait(barrier, 8)

    def halo_to(i, dp):
        return remote(
            hb_first.at[pl.ds(4, 4)], hb_first.at[pl.ds((1 - dp) * 4, 4)], s_h.at[i], r_h.at[i],
            z_peer(dp),
        )

    def maps_to(i, dp):
        return remote(
            seg_out.at[pl.ds(3, 2)], de.at[1 - dp], s_d.at[i], r_d.at[i], z_peer(dp)
        )

    sides = ((0, 1), (1, -1))
    for side in sides:
        sends.append(lambda side=side: halo_to(*side))
        sends.append(lambda side=side: maps_to(*side))

    for side in sides:
        halo_to(*side).start()
    maps0 = send_maps(0)
    local[3].wait()
    local[4].wait()
    for n in range(4):
        eb[n, :B, :B] = dot3(element(di, n, 0), element(up, n, 0))
        seg_out[4, n, :B, :B] = dot3(element(di, n, 1), element(up, n, 1))
        seg_out[1, n, :B, :B] = dot3(eb[n, :B, :B], own(4, n))
    maps1 = send_maps(1)
    for n in range(4):
        wb[n, :B, :B] = dot3(eb[n, :B, :B], element(di, n, 1))
        whole = dot3(element(di, n, 0), element(lo, n, 0)) + dot3(wb[n, :B, :B], own(0, n))
        seg_out[2, n, :B, :B] = -whole
    maps2 = send_maps(2)
    for n in range(4):
        seg_out[3, n, :B, :B] = element(di, n, 1)

    for side in sides:
        maps_to(*side).start()
    for k in (5, 6, 7):
        local[k].wait()
    lhs[:, Q:] = jnp.zeros((8, 8), F32)
    for row in range(8):
        high, rest = split(
            jnp.concatenate([fo[row // 2, row % 2], jnp.zeros((8, B), F32)], axis=0)
        )
        wfc[row, :, :B] = high
        wfc[row, :, 128 : 128 + B] = rest

    for side in sides:
        halo_to(*side).wait_recv()
    first_in = send_local(0, right_sides(0))
    def send_entries(j, d):
        return [
            remote(
                ent_out.at[j, 0], ent_in.at[y, 1 - dp], s_t.at[dp + 1, d], r_t.at[dp + 1, d],
                at(d, dp),
            )
            for dp in ((-1, 1, 0) if d else (-1, 1))
        ]

    def store_entries(ref, done):
        for c in both:
            for j in range(4):
                for row in range(3):
                    ref[j, c, row : row + 1, :B] = done[c][row][j]

    maps0()
    p01 = [dot3(seg(c, 0, 1), seg(c, 0, 0)) for c in both]
    p23 = [dot3(seg(c, 0, 3), seg(c, 0, 2)) for c in both]
    for c in both:
        part[c, 0, :B, :B] = p01[c]
    quarters0 = send_quarter(0, [dot3(p23[c], p01[c]) for c in both])
    maps1()
    n01 = [dot3(seg(c, 1, 0), seg(c, 1, 1)) for c in both]
    n23 = [dot3(seg(c, 1, 2), seg(c, 1, 3)) for c in both]
    for c in both:
        part[c, 5, :B, :B] = n23[c]
    quarters1 = send_quarter(1, [dot3(n01[c], n23[c]) for c in both])
    maps2()
    k1m0 = [dot3(seg(c, 2, 1), seg(c, 0, 0)) for c in both]
    k01 = [seg(c, 2, 0) + dot3(seg(c, 1, 0), k1m0[c]) for c in both]
    k23 = [
        seg(c, 2, 2) + dot3(seg(c, 1, 2), dot3(seg(c, 2, 3), seg(c, 0, 2))) for c in both
    ]
    quarters2 = send_quarter(
        2, [k01[c] + dot3(n01[c], dot3(k23[c], p01[c])) for c in both]
    )
    first_in()
    starts = quarter_tails(0)
    vectors, ends = send_quarter_vectors(0, starts)
    for c in both:
        p3 = dot3(seg(c, 0, 2), p01[c])
        part[c, 1, :B, :B] = p3
        k2 = dot3(seg(c, 2, 3), p3)
        part[c, 2, :B, :B] = k2
        k1 = dot3(seg(c, 2, 2), p01[c]) + dot3(seg(c, 1, 2), k2)
        part[c, 3, :B, :B] = k1
        part[c, 4, :B, :B] = k1m0[c] + dot3(seg(c, 1, 1), k1)
        part[c, 6, :B, :B] = dot3(seg(c, 1, 1), n23[c])
    quarters0()
    quarters1()
    quarters2()
    vectors()
    done = fields(0, starts, ends)
    store_entries(ent_out, done)
    for d in (2, 1, 3, 0):
        for copy in send_entries(ys[d], d):
            copy.start()
    ent_in[y, 1] = ent_out[y, 0]

    for side in sides:
        maps_to(*side).wait_recv()
    for d in (0, 1, 3, 2):
        for copy in send_entries(0, d):
            copy.wait_recv()

    for o in range(3):
        for n in range(4):
            row = 8 * o + 2 * n
            entry = ent_in[n, o]
            if o == 1:
                pivot, upper = own(3, n), own(4, n)
            else:
                pivot, upper = de[o, 0, n, :B, :B], de[o, 1, n, :B, :B]
            f24[row : row + 1, :] = entry[0:1, :B]
            f24[row + 1 : row + 2, :] = apply2(pivot, entry[1:2, :B], upper, -entry[2:3, :B])
    halo = dot3(f24[...], rst[...], NT)
    for m in range(12):
        hb_second[m, :, :Q] = halo[2 * m : 2 * m + 2]
    second_in = send_local(1, right_sides(1))

    def send_field(d):
        return remote(fx.at[ys[d], 0], ob.at[y], s_f.at[d], r_f.at[d], at(d))

    second_in()
    starts = quarter_tails(1)
    vectors, ends = send_quarter_vectors(1, starts)
    vectors()
    done = fields(1, starts, ends)
    store_entries(fx, done)
    for d in (2, 1, 3):
        send_field(d).start()
    ob[y] = fx[y, 0]

    for d in (1, 3, 2):
        send_field(d).wait_recv()

    for n in range(4):
        entry = ob[n]
        out[2 * n : 2 * n + 1, :] = entry[0:1, :B]
        out[2 * n + 1 : 2 * n + 2, :] = apply2(
            own(3, n), entry[1:2, :B], own(4, n), -entry[2:3, :B]
        )
    for make in sends:
        make().wait_send()

    for d in range(4):
        for copy in send_entries(0, d):
            copy.wait_send()
        if d:
            send_field(d).wait_send()


def per_device(residual, previous, lower, pivot, upper, couple, restrict, neighbours):
    def factor(a):
        return jnp.transpose(a, (0, 2, 1, 3)).reshape(4, 2 * B, B)

    dma = pltpu.SemaphoreType.DMA
    result = pl.pallas_call(
        kernel,
        out_shape=jax.ShapeDtypeStruct((8, B), F32),
        in_specs=[pl.BlockSpec(memory_space=pl.ANY)] * 8,
        out_specs=pl.BlockSpec(memory_space=pltpu.VMEM),
        scratch_shapes=[
            pltpu.SMEM((4, 4), jnp.int32),
            pltpu.VMEM((8, B), F32),
            pltpu.VMEM((8, B), F32),
            pltpu.VMEM((Q, B), F32),
            pltpu.VMEM((4, 2 * B, B), F32),
            pltpu.VMEM((4, 2 * B, B), F32),
            pltpu.VMEM((4, 2 * B, B), F32),
            pltpu.VMEM((4, 2, Q, B), F32),
            pltpu.VMEM((8, Q + 8, 256), BF16),
            pltpu.VMEM((4, 104, 128), F32),
            pltpu.VMEM((4, 104, 128), F32),
            pltpu.VMEM((5, 4, 104, 128), F32),
            pltpu.VMEM((1, 3, 4, 104, 128), F32),
            pltpu.VMEM((4, 3, 1, 104, 128), F32),
            pltpu.VMEM((1, 7, 104, 128), F32),
            pltpu.VMEM((3, 2, 4, 104, 128), F32),
            pltpu.VMEM((12, 2, 256), F32),
            pltpu.VMEM((12, 2, 256), F32),
            pltpu.VMEM((8, Q + 8), F32),
            pltpu.VMEM((24, B), F32),
            pltpu.VMEM((4, 1, 4, 128), F32),
            pltpu.VMEM((4, 3, 4, 128), F32),
            pltpu.VMEM((2, 4, 2, 128), F32),
            pltpu.VMEM((2, 1, 4, 2, 128), F32),
            pltpu.VMEM((2, 4, 1, 2, 128), F32),
            pltpu.VMEM((4, 1, 4, 128), F32),
            pltpu.VMEM((4, 4, 128), F32),
            dma((8,)),
            dma((2,)),
            dma((2,)),
            dma((3, 4)),
            dma((1, 3, 4)),
            dma((3, 4)),
            dma((3, 4)),
            dma((2,)),
            dma((2,)),
            dma((2, 4)),
            dma((2, 1, 4)),
            dma((2, 4)),
            dma((2, 4)),
            dma((3, 4)),
            dma((3, 4)),
            dma((4,)),
            dma((4,)),
        ],
        compiler_params=pltpu.CompilerParams(
            collective_id=0, has_side_effects=True, vmem_limit_bytes=60 << 20
        ),
    )(
        neighbours,
        residual.reshape(8, B),
        previous.reshape(8, B),
        jnp.transpose(restrict, (1, 0, 2)).reshape(Q, B),
        factor(lower),
        factor(pivot),
        factor(upper),
        jnp.transpose(couple, (0, 1, 4, 2, 3)).reshape(4, 2, Q, B),
    )
    return result.reshape(4, 2, B)


def solution(mesh):
    placed = (
        P("patch", "line", None),
        P("patch", "line", None),
        P("patch", "line", None, None),
        P("patch", "line", None, None),
        P("patch", "line", None, None),
        P("patch", "line", None, None, None),
        P(),
        P("patch", None),
    )
    return jax.shard_map(
        per_device, mesh=mesh, in_specs=placed, out_specs=P("patch", "line", None), check_vma=False
    )
```

```python
import jax
import jax.numpy as jnp
from jax import lax
from jax.experimental import pallas as pl
from jax.experimental.pallas import tpu as pltpu
from jax.sharding import PartitionSpec as P

F32 = jnp.float32
BF16 = jnp.bfloat16
MESH = pl.DeviceIdType.MESH
B = 100
Q = 200
NP = 32
NN = (((1,), (0,)), ((), ()))
NT = (((1,), (1,)), ((), ()))


def split(a):
    high = a.astype(BF16)
    return high, (a - high.astype(F32)).astype(BF16)


def dot3(a, b, dims=NN):
    ah, al = split(a)
    bh, bl = split(b)

    def mm(u, v):
        return lax.dot_general(u, v, dims, preferred_element_type=F32)

    return mm(ah, bh) + (mm(ah, bl) + mm(al, bh))


def kernel(
    nb_any, res_any, prev_any, rst_any, low, piv, upp, fc, out,
    nb, res, prev, rst, lo, di, up, fo, wfc,
    eb, wb, seg_out, seg_in, quarter, part, de, hb_first, hb_second, lhs, f24, ent_out, ent_in,
    a_out, a_in, th, fx, ob,
    s_loc, s_d, r_d, s_m, r_m, s_q, r_q, s_h, r_h, s_a, r_a, s_x, r_x, s_t, r_t, s_f, r_f,
):
    p = lax.axis_index("patch")
    line = lax.axis_index("line")
    x, y = line // 4, line % 4
    ys = [(y + d) % 4 for d in range(4)]

    def at(d, dp=0):
        return ((p + dp + NP) % NP, x * 4 + ys[d])

    def x_peer(d):
        return (p, ((x + d) % 4) * 4 + y)

    def z_peer(d):
        return ((p + d + NP) % NP, line)

    def remote(src, dst, send, recv, device):
        return pltpu.make_async_remote_copy(
            src_ref=src, dst_ref=dst, send_sem=send, recv_sem=recv,
            device_id=device, device_id_type=MESH,
        )

    barrier = pltpu.get_barrier_semaphore()

    def greet(device):
        pl.semaphore_signal(barrier, inc=1, device_id=device, device_id_type=MESH)

    for d in (2, 1, 3):
        greet(at(d))
        greet(x_peer(d))
    greet(at(0, 1))
    greet(at(0, -1))
    pairs = (
        (low, lo), (prev_any, prev), (rst_any, rst), (piv, di), (upp, up),
        (nb_any, nb), (res_any, res), (fc, fo),
    )
    local = [
        pltpu.make_async_copy(src, dst, s_loc.at[k]) for k, (src, dst) in enumerate(pairs)
    ]
    for copy in local:
        copy.start()

    hb = (hb_first, hb_second)
    sends = []
    eye = lax.broadcasted_iota(jnp.int32, (B, B), 0) == lax.broadcasted_iota(
        jnp.int32, (B, B), 1
    )

    def to_row(column):
        return jnp.sum(jnp.where(eye, column, 0.0), axis=0, keepdims=True)

    def apply(matrix, row):
        return to_row(jnp.sum(matrix * row, axis=1, keepdims=True))

    def apply2(one, u, two, v):
        return to_row(jnp.sum(one * u + two * v, axis=1, keepdims=True))

    def element(ref, n, l):
        return ref[n, pl.ds(l, B, stride=2), :]

    def own(k, n):
        return seg_out[k, n, :B, :B]

    def to_owner(src, dst, send, recv):
        def make(d):
            return remote(src(ys[d]), dst(0, y), send.at[d], recv(0, d), at(d))

        for d in (2, 1, 3):
            make(d).start()
            sends.append(lambda d=d: make(d))
        dst(0, y)[...] = src(y)[...]

        def arrived():
            for d in (1, 3, 2):
                make(d).wait_recv()

        return arrived

    def send_maps(k):
        return to_owner(
            lambda n: seg_out.at[k, n], lambda c, j: seg_in.at[c, k, j], s_m.at[k],
            lambda c, d: r_m.at[c, k, d],
        )

    lane = lax.broadcasted_iota(jnp.int32, (2, Q), 1) % 4

    def pick(block, source, f):
        total = jnp.zeros(block.shape, F32)
        for g in range(4):
            moved = block if g == f else pltpu.roll(block, (f - g) % 256, axis=1)
            total = jnp.where(source == g, moved, total)
        return jnp.where(lane == f, total[:, :Q], 0.0)

    def right_sides(sweep):
        for n in range(4):
            picked = jnp.zeros((2, Q), F32)
            for f in range(4):
                entry = nb[n, f]
                picked = picked + pick(
                    hb[sweep][entry // 4], entry % 4, f
                )
            lhs[2 * n : 2 * n + 2, :Q] = picked
        whole = lhs[...]
        high = whole.astype(BF16).astype(F32)
        halves = jnp.concatenate([high, whole - high], axis=0).astype(BF16)
        rows = []
        for row in range(8):
            got = lax.dot_general(halves, wfc[row], NN, preferred_element_type=F32)
            low = got[row : row + 1, 128 : 128 + B] + got[row + 8 : row + 9, :B]
            rows.append(res[row : row + 1, :] - (got[row : row + 1, :B] + low))
        return rows

    def send_local(sweep, rows):
        tails = []
        for n in range(4):
            tails.append(rows[2 * n + 1] - apply(element(lo, n, 1), rows[2 * n]))
        for n in range(4):
            a_out[sweep, n, 0:1, :B] = tails[n]
            a_out[sweep, n, 1:2, :B] = apply2(
                element(di, n, 0), rows[2 * n], wb[n, :B, :B], -tails[n]
            )
        return to_owner(
            lambda n: a_out.at[sweep, n], lambda c, j: a_in.at[sweep, c, j], s_a.at[sweep],
            lambda c, d: r_a.at[sweep, c, d],
        )

    both = (0,)

    def seg(c, k, j):
        return seg_in[c, k, j, :B, :B]

    def q(c, j, k):
        return quarter[j, k, c, :B, :B]

    def across(make):
        for d in (2, 1, 3):
            make(d).start()
            sends.append(lambda d=d: make(d))

        def arrived():
            for d in (1, 3, 2):
                make(d).wait_recv()

        return arrived

    def send_quarter(k, values):
        for c in both:
            quarter[x, k, c, :B, :B] = values[c]
        return across(
            lambda d: remote(
                quarter.at[x, k], quarter.at[x, k], s_q.at[k, d], r_q.at[k, d], x_peer(d)
            )
        )

    def quarter_tails(sweep):
        tails = [[a_in[sweep, c, j, 0:1, :B] for j in range(4)] for c in both]
        y2 = [tails[c][1] + apply(seg(c, 0, 1), tails[c][0]) for c in both]
        y3 = [tails[c][2] + apply(seg(c, 0, 2), y2[c]) for c in both]
        last = [tails[c][3] + apply(seg(c, 0, 3), y3[c]) for c in both]
        return [(None, tails[c][0], y2[c], y3[c], last[c]) for c in both]

    def send_quarter_vectors(sweep, starts):
        heads = [[a_in[sweep, c, j, 1:2, :B] for j in range(4)] for c in both]
        ends = [[None, None, None, h[3]] for h in heads]
        g3 = [heads[c][3] + apply(seg(c, 2, 3), starts[c][3]) for c in both]
        g2 = [
            heads[c][2] + apply2(seg(c, 2, 2), starts[c][2], seg(c, 1, 2), g3[c]) for c in both
        ]
        g1 = [
            heads[c][1] + apply2(seg(c, 2, 1), starts[c][1], seg(c, 1, 1), g2[c]) for c in both
        ]
        g0 = [heads[c][0] + apply(seg(c, 1, 0), g1[c]) for c in both]
        for c in both:
            th[sweep, x, c, 0:1, :B] = starts[c][4]
            th[sweep, x, c, 1:2, :B] = g0[c]
        arrived = across(
            lambda d: remote(
                th.at[sweep, x], th.at[sweep, x], s_x.at[sweep, d], r_x.at[sweep, d], x_peer(d)
            )
        )
        return arrived, [(g0[c], g1[c], g2[c], g3[c]) for c in both]

    def mine(values):
        total = values[0]
        for j in range(1, 4):
            total = jnp.where(x == j, values[j], total)
        return total

    def fields(sweep, starts, ends):
        tail = [[th[sweep, j, c, 0:1, :B] for j in range(4)] for c in both]
        head = [[th[sweep, j, c, 1:2, :B] for j in range(4)] for c in both]
        zero = jnp.zeros((1, B), F32)
        y2 = [tail[c][1] + apply(q(c, 1, 0), tail[c][0]) for c in both]
        y3 = [tail[c][2] + apply(q(c, 2, 0), y2[c]) for c in both]
        h3 = [head[c][3] + apply(q(c, 3, 2), y3[c]) for c in both]
        h2 = [head[c][2] + apply2(q(c, 2, 2), y2[c], q(c, 2, 1), h3[c]) for c in both]
        h1 = [head[c][1] + apply2(q(c, 1, 2), tail[c][0], q(c, 1, 1), h2[c]) for c in both]
        result = []
        for c in both:
            y_in = mine((zero, tail[c][0], y2[c], y3[c]))
            x_in = mine((h1[c], h2[c], h3[c], zero))
            ahead = [
                starts[c][1] + apply(seg(c, 0, 0), y_in),
                starts[c][2] + apply(part[c, 0, :B, :B], y_in),
                starts[c][3] + apply(part[c, 1, :B, :B], y_in),
                starts[c][4] + apply(quarter[x, 0, c, :B, :B], y_in),
            ]
            g0, g1, g2, g3 = ends[c]
            first = [
                g0 + apply2(quarter[x, 2, c, :B, :B], y_in, quarter[x, 1, c, :B, :B], x_in),
                g1 + apply2(part[c, 4, :B, :B], y_in, part[c, 6, :B, :B], x_in),
                g2 + apply2(part[c, 3, :B, :B], y_in, part[c, 5, :B, :B], x_in),
                g3 + apply2(part[c, 2, :B, :B], y_in, seg(c, 1, 3), x_in),
            ]
            behind = first[1:] + [x_in]
            result.append((first, ahead, behind))
        return result

    local[0].wait()
    for n in range(4):
        seg_out[0, n, :B, :B] = dot3(element(lo, n, 1), element(lo, n, 0))
    local[1].wait()
    local[2].wait()
    halo = dot3(prev[...], rst[...], NT)
    for n in range(4):
        hb_first[4 + n, :, :Q] = halo[2 * n : 2 * n + 2]

    pl.semaphore_wait(barrier, 8)

    def halo_to(i, dp):
        return remote(
            hb_first.at[pl.ds(4, 4)], hb_first.at[pl.ds((1 - dp) * 4, 4)], s_h.at[i], r_h.at[i],
            z_peer(dp),
        )

    def maps_to(i, dp):
        return remote(
            seg_out.at[pl.ds(3, 2)], de.at[1 - dp], s_d.at[i], r_d.at[i], z_peer(dp)
        )

    sides = ((0, 1), (1, -1))
    for side in sides:
        sends.append(lambda side=side: halo_to(*side))
        sends.append(lambda side=side: maps_to(*side))

    for side in sides:
        halo_to(*side).start()
    maps0 = send_maps(0)
    local[3].wait()
    local[4].wait()
    for n in range(4):
        eb[n, :B, :B] = dot3(element(di, n, 0), element(up, n, 0))
        seg_out[4, n, :B, :B] = dot3(element(di, n, 1), element(up, n, 1))
        seg_out[1, n, :B, :B] = dot3(eb[n, :B, :B], own(4, n))
    maps1 = send_maps(1)
    for n in range(4):
        wb[n, :B, :B] = dot3(eb[n, :B, :B], element(di, n, 1))
        whole = dot3(element(di, n, 0), element(lo, n, 0)) + dot3(wb[n, :B, :B], own(0, n))
        seg_out[2, n, :B, :B] = -whole
    maps2 = send_maps(2)
    for n in range(4):
        seg_out[3, n, :B, :B] = element(di, n, 1)

    for k in (5, 6, 7):
        local[k].wait()
    lhs[:, Q:] = jnp.zeros((8, 8), F32)
    for row in range(8):
        high, rest = split(
            jnp.concatenate([fo[row // 2, row % 2], jnp.zeros((8, B), F32)], axis=0)
        )
        wfc[row, :, :B] = high
        wfc[row, :, 128 : 128 + B] = rest

    for side in sides:
        halo_to(*side).wait_recv()
    first_in = send_local(0, right_sides(0))
    def send_entries(j, d, steps=(-1, 1, 0)):
        return [
            remote(
                ent_out.at[j, 0], ent_in.at[y, 1 - dp], s_t.at[dp + 1, d], r_t.at[dp + 1, d],
                at(d, dp),
            )
            for dp in steps
            if d or dp
        ]

    def store_entries(ref, done):
        for c in both:
            for j in range(4):
                for row in range(3):
                    ref[j, c, row : row + 1, :B] = done[c][row][j]

    maps0()
    p01 = [dot3(seg(c, 0, 1), seg(c, 0, 0)) for c in both]
    p23 = [dot3(seg(c, 0, 3), seg(c, 0, 2)) for c in both]
    for c in both:
        part[c, 0, :B, :B] = p01[c]
    quarters0 = send_quarter(0, [dot3(p23[c], p01[c]) for c in both])
    maps1()
    n01 = [dot3(seg(c, 1, 0), seg(c, 1, 1)) for c in both]
    n23 = [dot3(seg(c, 1, 2), seg(c, 1, 3)) for c in both]
    for c in both:
        part[c, 5, :B, :B] = n23[c]
    quarters1 = send_quarter(1, [dot3(n01[c], n23[c]) for c in both])
    for side in sides:
        maps_to(*side).start()
    p3 = [dot3(seg(c, 0, 2), p01[c]) for c in both]
    n02 = [dot3(n01[c], seg(c, 1, 2)) for c in both]
    for c in both:
        part[c, 1, :B, :B] = p3[c]
        part[c, 6, :B, :B] = dot3(seg(c, 1, 1), n23[c])
    maps2()
    k1m0 = [dot3(seg(c, 2, 1), seg(c, 0, 0)) for c in both]
    k2m1 = [dot3(seg(c, 2, 2), p01[c]) for c in both]
    k3m2 = [dot3(seg(c, 2, 3), p3[c]) for c in both]
    quarters2 = send_quarter(
        2,
        [
            (seg(c, 2, 0) + dot3(seg(c, 1, 0), k1m0[c]))
            + (dot3(n01[c], k2m1[c]) + dot3(n02[c], k3m2[c]))
            for c in both
        ],
    )
    first_in()
    starts = quarter_tails(0)
    vectors, ends = send_quarter_vectors(0, starts)
    for c in both:
        part[c, 2, :B, :B] = k3m2[c]
        k1 = k2m1[c] + dot3(seg(c, 1, 2), k3m2[c])
        part[c, 3, :B, :B] = k1
        part[c, 4, :B, :B] = k1m0[c] + dot3(seg(c, 1, 1), k1)
    quarters0()
    quarters1()
    quarters2()
    vectors()
    done = fields(0, starts, ends)
    store_entries(ent_out, done)
    for d in (2, 1, 3, 0):
        for copy in send_entries(ys[d], d):
            copy.start()
    ent_in[y, 1] = ent_out[y, 0]

    def second_elements(o):
        for n in range(4):
            row = 8 * o + 2 * n
            entry = ent_in[n, o]
            if o == 1:
                pivot, upper = own(3, n), own(4, n)
            else:
                pivot, upper = de[o, 0, n, :B, :B], de[o, 1, n, :B, :B]
            f24[row : row + 1, :] = entry[0:1, :B]
            f24[row + 1 : row + 2, :] = apply2(pivot, entry[1:2, :B], upper, -entry[2:3, :B])

    for side in sides:
        maps_to(*side).wait_recv()
    for d in (1, 3, 2):
        send_entries(0, d, (0,))[0].wait_recv()
    second_elements(1)
    for d in (0, 1, 3, 2):
        for copy in send_entries(0, d, (-1, 1)):
            copy.wait_recv()
    second_elements(0)
    second_elements(2)
    halo = dot3(f24[...], rst[...], NT)
    for m in range(12):
        hb_second[m, :, :Q] = halo[2 * m : 2 * m + 2]
    second_in = send_local(1, right_sides(1))

    def send_field(d):
        return remote(fx.at[ys[d], 0], ob.at[y], s_f.at[d], r_f.at[d], at(d))

    second_in()
    starts = quarter_tails(1)
    vectors, ends = send_quarter_vectors(1, starts)
    vectors()
    done = fields(1, starts, ends)
    store_entries(fx, done)
    for d in (2, 1, 3):
        send_field(d).start()
    ob[y] = fx[y, 0]

    for d in (1, 3, 2):
        send_field(d).wait_recv()

    for n in range(4):
        entry = ob[n]
        out[2 * n : 2 * n + 1, :] = entry[0:1, :B]
        out[2 * n + 1 : 2 * n + 2, :] = apply2(
            own(3, n), entry[1:2, :B], own(4, n), -entry[2:3, :B]
        )
    for make in sends:
        make().wait_send()

    for d in range(4):
        for copy in send_entries(0, d):
            copy.wait_send()
        if d:
            send_field(d).wait_send()


def per_device(residual, previous, lower, pivot, upper, couple, restrict, neighbours):
    def factor(a):
        return jnp.transpose(a, (0, 2, 1, 3)).reshape(4, 2 * B, B)

    dma = pltpu.SemaphoreType.DMA
    result = pl.pallas_call(
        kernel,
        out_shape=jax.ShapeDtypeStruct((8, B), F32),
        in_specs=[pl.BlockSpec(memory_space=pl.ANY)] * 8,
        out_specs=pl.BlockSpec(memory_space=pltpu.VMEM),
        scratch_shapes=[
            pltpu.SMEM((4, 4), jnp.int32),
            pltpu.VMEM((8, B), F32),
            pltpu.VMEM((8, B), F32),
            pltpu.VMEM((Q, B), F32),
            pltpu.VMEM((4, 2 * B, B), F32),
            pltpu.VMEM((4, 2 * B, B), F32),
            pltpu.VMEM((4, 2 * B, B), F32),
            pltpu.VMEM((4, 2, Q, B), F32),
            pltpu.VMEM((8, Q + 8, 256), BF16),
            pltpu.VMEM((4, 104, 128), F32),
            pltpu.VMEM((4, 104, 128), F32),
            pltpu.VMEM((5, 4, 104, 128), F32),
            pltpu.VMEM((1, 3, 4, 104, 128), F32),
            pltpu.VMEM((4, 3, 1, 104, 128), F32),
            pltpu.VMEM((1, 7, 104, 128), F32),
            pltpu.VMEM((3, 2, 4, 104, 128), F32),
            pltpu.VMEM((12, 2, 256), F32),
            pltpu.VMEM((12, 2, 256), F32),
            pltpu.VMEM((8, Q + 8), F32),
            pltpu.VMEM((24, B), F32),
            pltpu.VMEM((4, 1, 4, 128), F32),
            pltpu.VMEM((4, 3, 4, 128), F32),
            pltpu.VMEM((2, 4, 2, 128), F32),
            pltpu.VMEM((2, 1, 4, 2, 128), F32),
            pltpu.VMEM((2, 4, 1, 2, 128), F32),
            pltpu.VMEM((4, 1, 4, 128), F32),
            pltpu.VMEM((4, 4, 128), F32),
            dma((8,)),
            dma((2,)),
            dma((2,)),
            dma((3, 4)),
            dma((1, 3, 4)),
            dma((3, 4)),
            dma((3, 4)),
            dma((2,)),
            dma((2,)),
            dma((2, 4)),
            dma((2, 1, 4)),
            dma((2, 4)),
            dma((2, 4)),
            dma((3, 4)),
            dma((3, 4)),
            dma((4,)),
            dma((4,)),
        ],
        compiler_params=pltpu.CompilerParams(
            collective_id=0, has_side_effects=True, vmem_limit_bytes=60 << 20
        ),
    )(
        neighbours,
        residual.reshape(8, B),
        previous.reshape(8, B),
        jnp.transpose(restrict, (1, 0, 2)).reshape(Q, B),
        factor(lower),
        factor(pivot),
        factor(upper),
        jnp.transpose(couple, (0, 1, 4, 2, 3)).reshape(4, 2, Q, B),
    )
    return result.reshape(4, 2, B)


def solution(mesh):
    placed = (
        P("patch", "line", None),
        P("patch", "line", None),
        P("patch", "line", None, None),
        P("patch", "line", None, None),
        P("patch", "line", None, None),
        P("patch", "line", None, None, None),
        P(),
        P("patch", None),
    )
    return jax.shard_map(
        per_device, mesh=mesh, in_specs=placed, out_specs=P("patch", "line", None), check_vma=False
    )
```

```python
import jax
import jax.numpy as jnp
from jax import lax
from jax.experimental import pallas as pl
from jax.experimental.pallas import tpu as pltpu
from jax.sharding import PartitionSpec as P

F32 = jnp.float32
BF16 = jnp.bfloat16
MESH = pl.DeviceIdType.MESH
B = 100
Q = 200
NP = 32
NN = (((1,), (0,)), ((), ()))
NT = (((1,), (1,)), ((), ()))


def split(a):
    high = a.astype(BF16)
    return high, (a - high.astype(F32)).astype(BF16)


def dot3(a, b, dims=NN):
    ah, al = split(a)
    bh, bl = split(b)

    def mm(u, v):
        return lax.dot_general(u, v, dims, preferred_element_type=F32)

    return mm(ah, bh) + (mm(ah, bl) + mm(al, bh))


def kernel(
    nb_any, res_any, prev_any, rst_any, low, piv, upp, fc, out,
    nb, res, prev, rst, lo, di, up, fo, wfc,
    eb, wb, seg_out, seg_in, quarter, part, de, hb_first, hb_second, lhs, f24, ent_out, ent_in,
    a_out, a_in, th, fx, ob,
    s_loc, s_d, r_d, s_m, r_m, s_q, r_q, s_h, r_h, s_a, r_a, s_x, r_x, s_t, r_t, s_f, r_f,
):
    p = lax.axis_index("patch")
    line = lax.axis_index("line")
    x, y = line // 4, line % 4
    ys = [(y + d) % 4 for d in range(4)]

    def at(d, dp=0):
        return ((p + dp + NP) % NP, x * 4 + ys[d])

    def x_peer(d):
        return (p, ((x + d) % 4) * 4 + y)

    def z_peer(d):
        return ((p + d + NP) % NP, line)

    def remote(src, dst, send, recv, device):
        return pltpu.make_async_remote_copy(
            src_ref=src, dst_ref=dst, send_sem=send, recv_sem=recv,
            device_id=device, device_id_type=MESH,
        )

    barrier = pltpu.get_barrier_semaphore()

    def greet(device):
        pl.semaphore_signal(barrier, inc=1, device_id=device, device_id_type=MESH)

    for d in (2, 1, 3):
        greet(at(d))
        greet(x_peer(d))
    greet(at(0, 1))
    greet(at(0, -1))
    pairs = (
        (low, lo), (prev_any, prev), (rst_any, rst), (piv, di), (upp, up),
        (nb_any, nb), (res_any, res), (fc, fo),
    )
    local = [
        pltpu.make_async_copy(src, dst, s_loc.at[k]) for k, (src, dst) in enumerate(pairs)
    ]
    for copy in local:
        copy.start()

    hb = (hb_first, hb_second)
    sends = []
    eye = lax.broadcasted_iota(jnp.int32, (B, B), 0) == lax.broadcasted_iota(
        jnp.int32, (B, B), 1
    )

    def to_row(column):
        return jnp.sum(jnp.where(eye, column, 0.0), axis=0, keepdims=True)

    def apply(matrix, row):
        return to_row(jnp.sum(matrix * row, axis=1, keepdims=True))

    def apply2(one, u, two, v):
        return to_row(jnp.sum(one * u + two * v, axis=1, keepdims=True))

    def element(ref, n, l):
        return ref[n, pl.ds(l, B, stride=2), :]

    def own(k, n):
        return seg_out[k, n, :B, :B]

    def to_owner(src, dst, send, recv):
        def make(d):
            return remote(src(ys[d]), dst(0, y), send.at[d], recv(0, d), at(d))

        for d in (2, 1, 3):
            make(d).start()
            sends.append(lambda d=d: make(d))
        dst(0, y)[...] = src(y)[...]

        def arrived():
            for d in (1, 3, 2):
                make(d).wait_recv()

        return arrived

    def send_maps(k):
        return to_owner(
            lambda n: seg_out.at[k, n], lambda c, j: seg_in.at[c, k, j], s_m.at[k],
            lambda c, d: r_m.at[c, k, d],
        )

    lane = lax.broadcasted_iota(jnp.int32, (2, Q), 1) % 4

    def pick(block, source, f):
        total = jnp.zeros(block.shape, F32)
        for g in range(4):
            moved = block if g == f else pltpu.roll(block, (f - g) % 256, axis=1)
            total = jnp.where(source == g, moved, total)
        return jnp.where(lane == f, total[:, :Q], 0.0)

    def right_sides(sweep):
        for n in range(4):
            picked = jnp.zeros((2, Q), F32)
            for f in range(4):
                entry = nb[n, f]
                picked = picked + pick(
                    hb[sweep][entry // 4], entry % 4, f
                )
            lhs[2 * n : 2 * n + 2, :Q] = picked
        whole = lhs[...]
        high = whole.astype(BF16).astype(F32)
        halves = jnp.concatenate([high, whole - high], axis=0).astype(BF16)
        rows = []
        for row in range(8):
            got = lax.dot_general(halves, wfc[row], NN, preferred_element_type=F32)
            low = got[row : row + 1, 128 : 128 + B] + got[row + 8 : row + 9, :B]
            rows.append(res[row : row + 1, :] - (got[row : row + 1, :B] + low))
        return rows

    def send_local(sweep, rows):
        tails = []
        for n in range(4):
            tails.append(rows[2 * n + 1] - apply(element(lo, n, 1), rows[2 * n]))
        for n in range(4):
            a_out[sweep, n, 0:1, :B] = tails[n]
            a_out[sweep, n, 1:2, :B] = apply2(
                element(di, n, 0), rows[2 * n], wb[n, :B, :B], -tails[n]
            )
        return to_owner(
            lambda n: a_out.at[sweep, n], lambda c, j: a_in.at[sweep, c, j], s_a.at[sweep],
            lambda c, d: r_a.at[sweep, c, d],
        )

    both = (0,)

    def seg(c, k, j):
        return seg_in[c, k, j, :B, :B]

    def q(c, j, k):
        return quarter[j, k, c, :B, :B]

    def across(make):
        for d in (2, 1, 3):
            make(d).start()
            sends.append(lambda d=d: make(d))

        def arrived():
            for d in (1, 3, 2):
                make(d).wait_recv()

        return arrived

    def send_quarter(k, values):
        for c in both:
            quarter[x, k, c, :B, :B] = values[c]
        return across(
            lambda d: remote(
                quarter.at[x, k], quarter.at[x, k], s_q.at[k, d], r_q.at[k, d], x_peer(d)
            )
        )

    def quarter_tails(sweep):
        tails = [[a_in[sweep, c, j, 0:1, :B] for j in range(4)] for c in both]
        y2 = [tails[c][1] + apply(seg(c, 0, 1), tails[c][0]) for c in both]
        y3 = [tails[c][2] + apply(seg(c, 0, 2), y2[c]) for c in both]
        last = [tails[c][3] + apply(seg(c, 0, 3), y3[c]) for c in both]
        return [(None, tails[c][0], y2[c], y3[c], last[c]) for c in both]

    def send_quarter_vectors(sweep, starts):
        heads = [[a_in[sweep, c, j, 1:2, :B] for j in range(4)] for c in both]
        ends = [[None, None, None, h[3]] for h in heads]
        g3 = [heads[c][3] + apply(seg(c, 2, 3), starts[c][3]) for c in both]
        g2 = [
            heads[c][2] + apply2(seg(c, 2, 2), starts[c][2], seg(c, 1, 2), g3[c]) for c in both
        ]
        g1 = [
            heads[c][1] + apply2(seg(c, 2, 1), starts[c][1], seg(c, 1, 1), g2[c]) for c in both
        ]
        g0 = [heads[c][0] + apply(seg(c, 1, 0), g1[c]) for c in both]
        for c in both:
            th[sweep, x, c, 0:1, :B] = starts[c][4]
            th[sweep, x, c, 1:2, :B] = g0[c]
        arrived = across(
            lambda d: remote(
                th.at[sweep, x], th.at[sweep, x], s_x.at[sweep, d], r_x.at[sweep, d], x_peer(d)
            )
        )
        return arrived, [(g0[c], g1[c], g2[c], g3[c]) for c in both]

    def mine(values):
        total = values[0]
        for j in range(1, 4):
            total = jnp.where(x == j, values[j], total)
        return total

    def fields(sweep, starts, ends):
        tail = [[th[sweep, j, c, 0:1, :B] for j in range(4)] for c in both]
        head = [[th[sweep, j, c, 1:2, :B] for j in range(4)] for c in both]
        zero = jnp.zeros((1, B), F32)
        y2 = [tail[c][1] + apply(q(c, 1, 0), tail[c][0]) for c in both]
        y3 = [tail[c][2] + apply(q(c, 2, 0), y2[c]) for c in both]
        h3 = [head[c][3] + apply(q(c, 3, 2), y3[c]) for c in both]
        h2 = [head[c][2] + apply2(q(c, 2, 2), y2[c], q(c, 2, 1), h3[c]) for c in both]
        h1 = [head[c][1] + apply2(q(c, 1, 2), tail[c][0], q(c, 1, 1), h2[c]) for c in both]
        result = []
        for c in both:
            y_in = mine((zero, tail[c][0], y2[c], y3[c]))
            x_in = mine((h1[c], h2[c], h3[c], zero))
            ahead = [
                starts[c][1] + apply(seg(c, 0, 0), y_in),
                starts[c][2] + apply(part[c, 0, :B, :B], y_in),
                starts[c][3] + apply(part[c, 1, :B, :B], y_in),
                starts[c][4] + apply(quarter[x, 0, c, :B, :B], y_in),
            ]
            g0, g1, g2, g3 = ends[c]
            first = [
                g0 + apply2(quarter[x, 2, c, :B, :B], y_in, quarter[x, 1, c, :B, :B], x_in),
                g1 + apply2(part[c, 4, :B, :B], y_in, part[c, 6, :B, :B], x_in),
                g2 + apply2(part[c, 3, :B, :B], y_in, part[c, 5, :B, :B], x_in),
                g3 + apply2(part[c, 2, :B, :B], y_in, seg(c, 1, 3), x_in),
            ]
            behind = first[1:] + [x_in]
            result.append((first, ahead, behind))
        return result

    local[0].wait()
    for n in range(4):
        seg_out[0, n, :B, :B] = dot3(element(lo, n, 1), element(lo, n, 0))
    local[1].wait()
    local[2].wait()
    halo = dot3(prev[...], rst[...], NT)
    for n in range(4):
        hb_first[4 + n, :, :Q] = halo[2 * n : 2 * n + 2]

    pl.semaphore_wait(barrier, 8)

    def halo_to(i, dp):
        return remote(
            hb_first.at[pl.ds(4, 4)], hb_first.at[pl.ds((1 - dp) * 4, 4)], s_h.at[i], r_h.at[i],
            z_peer(dp),
        )

    def maps_to(i, dp):
        return remote(
            seg_out.at[pl.ds(3, 2)], de.at[1 - dp], s_d.at[i], r_d.at[i], z_peer(dp)
        )

    sides = ((0, 1), (1, -1))
    for side in sides:
        sends.append(lambda side=side: halo_to(*side))
        sends.append(lambda side=side: maps_to(*side))

    for side in sides:
        halo_to(*side).start()
    maps0 = send_maps(0)
    local[3].wait()
    local[4].wait()
    for n in range(4):
        eb[n, :B, :B] = dot3(element(di, n, 0), element(up, n, 0))
        seg_out[4, n, :B, :B] = dot3(element(di, n, 1), element(up, n, 1))
        seg_out[1, n, :B, :B] = dot3(eb[n, :B, :B], own(4, n))
    maps1 = send_maps(1)
    for n in range(4):
        wb[n, :B, :B] = dot3(eb[n, :B, :B], element(di, n, 1))
        whole = dot3(element(di, n, 0), element(lo, n, 0)) + dot3(wb[n, :B, :B], own(0, n))
        seg_out[2, n, :B, :B] = -whole
    maps2 = send_maps(2)
    for n in range(4):
        seg_out[3, n, :B, :B] = element(di, n, 1)

    for side in sides:
        maps_to(*side).start()
    for k in (5, 6, 7):
        local[k].wait()
    lhs[:, Q:] = jnp.zeros((8, 8), F32)
    for row in range(8):
        high, rest = split(
            jnp.concatenate([fo[row // 2, row % 2], jnp.zeros((8, B), F32)], axis=0)
        )
        wfc[row, :, :B] = high
        wfc[row, :, 128 : 128 + B] = rest

    for side in sides:
        halo_to(*side).wait_recv()
    first_in = send_local(0, right_sides(0))
    def send_entries(j, d, steps=(-1, 1, 0)):
        return [
            remote(
                ent_out.at[j, 0], ent_in.at[y, 1 - dp], s_t.at[dp + 1, d], r_t.at[dp + 1, d],
                at(d, dp),
            )
            for dp in steps
            if d or dp
        ]

    def store_entries(ref, done):
        for c in both:
            for j in range(4):
                for row in range(3):
                    ref[j, c, row : row + 1, :B] = done[c][row][j]

    maps0()
    p01 = [dot3(seg(c, 0, 1), seg(c, 0, 0)) for c in both]
    p23 = [dot3(seg(c, 0, 3), seg(c, 0, 2)) for c in both]
    for c in both:
        part[c, 0, :B, :B] = p01[c]
    quarters0 = send_quarter(0, [dot3(p23[c], p01[c]) for c in both])
    maps1()
    n01 = [dot3(seg(c, 1, 0), seg(c, 1, 1)) for c in both]
    n23 = [dot3(seg(c, 1, 2), seg(c, 1, 3)) for c in both]
    for c in both:
        part[c, 5, :B, :B] = n23[c]
    quarters1 = send_quarter(1, [dot3(n01[c], n23[c]) for c in both])
    p3 = [dot3(seg(c, 0, 2), p01[c]) for c in both]
    n02 = [dot3(n01[c], seg(c, 1, 2)) for c in both]
    for c in both:
        part[c, 1, :B, :B] = p3[c]
        part[c, 6, :B, :B] = dot3(seg(c, 1, 1), n23[c])
    maps2()
    k1m0 = [dot3(seg(c, 2, 1), seg(c, 0, 0)) for c in both]
    k2m1 = [dot3(seg(c, 2, 2), p01[c]) for c in both]
    k3m2 = [dot3(seg(c, 2, 3), p3[c]) for c in both]
    quarters2 = send_quarter(
        2,
        [
            (seg(c, 2, 0) + dot3(seg(c, 1, 0), k1m0[c]))
            + (dot3(n01[c], k2m1[c]) + dot3(n02[c], k3m2[c]))
            for c in both
        ],
    )
    first_in()
    starts = quarter_tails(0)
    vectors, ends = send_quarter_vectors(0, starts)
    for c in both:
        part[c, 2, :B, :B] = k3m2[c]
        k1 = k2m1[c] + dot3(seg(c, 1, 2), k3m2[c])
        part[c, 3, :B, :B] = k1
        part[c, 4, :B, :B] = k1m0[c] + dot3(seg(c, 1, 1), k1)
    quarters0()
    quarters1()
    quarters2()
    vectors()
    done = fields(0, starts, ends)
    store_entries(ent_out, done)
    for d in (2, 1, 3, 0):
        for copy in send_entries(ys[d], d):
            copy.start()
    ent_in[y, 1] = ent_out[y, 0]

    def second_elements(o):
        for n in range(4):
            row = 8 * o + 2 * n
            entry = ent_in[n, o]
            if o == 1:
                pivot, upper = own(3, n), own(4, n)
            else:
                pivot, upper = de[o, 0, n, :B, :B], de[o, 1, n, :B, :B]
            f24[row : row + 1, :] = entry[0:1, :B]
            f24[row + 1 : row + 2, :] = apply2(pivot, entry[1:2, :B], upper, -entry[2:3, :B])

    for side in sides:
        maps_to(*side).wait_recv()
    for d in (1, 3, 2):
        send_entries(0, d, (0,))[0].wait_recv()
    second_elements(1)
    for d in (0, 1, 3, 2):
        for copy in send_entries(0, d, (-1, 1)):
            copy.wait_recv()
    second_elements(0)
    second_elements(2)
    halo = dot3(f24[...], rst[...], NT)
    for m in range(12):
        hb_second[m, :, :Q] = halo[2 * m : 2 * m + 2]
    second_in = send_local(1, right_sides(1))

    def send_field(d):
        return remote(fx.at[ys[d], 0], ob.at[y], s_f.at[d], r_f.at[d], at(d))

    second_in()
    starts = quarter_tails(1)
    vectors, ends = send_quarter_vectors(1, starts)
    vectors()
    done = fields(1, starts, ends)
    store_entries(fx, done)
    for d in (2, 1, 3):
        send_field(d).start()
    ob[y] = fx[y, 0]

    for d in (1, 3, 2):
        send_field(d).wait_recv()

    for n in range(4):
        entry = ob[n]
        out[2 * n : 2 * n + 1, :] = entry[0:1, :B]
        out[2 * n + 1 : 2 * n + 2, :] = apply2(
            own(3, n), entry[1:2, :B], own(4, n), -entry[2:3, :B]
        )
    for make in sends:
        make().wait_send()

    for d in range(4):
        for copy in send_entries(0, d):
            copy.wait_send()
        if d:
            send_field(d).wait_send()


def per_device(residual, previous, lower, pivot, upper, couple, restrict, neighbours):
    def factor(a):
        return jnp.transpose(a, (0, 2, 1, 3)).reshape(4, 2 * B, B)

    dma = pltpu.SemaphoreType.DMA
    result = pl.pallas_call(
        kernel,
        out_shape=jax.ShapeDtypeStruct((8, B), F32),
        in_specs=[pl.BlockSpec(memory_space=pl.ANY)] * 8,
        out_specs=pl.BlockSpec(memory_space=pltpu.VMEM),
        scratch_shapes=[
            pltpu.SMEM((4, 4), jnp.int32),
            pltpu.VMEM((8, B), F32),
            pltpu.VMEM((8, B), F32),
            pltpu.VMEM((Q, B), F32),
            pltpu.VMEM((4, 2 * B, B), F32),
            pltpu.VMEM((4, 2 * B, B), F32),
            pltpu.VMEM((4, 2 * B, B), F32),
            pltpu.VMEM((4, 2, Q, B), F32),
            pltpu.VMEM((8, Q + 8, 256), BF16),
            pltpu.VMEM((4, 104, 128), F32),
            pltpu.VMEM((4, 104, 128), F32),
            pltpu.VMEM((5, 4, 104, 128), F32),
            pltpu.VMEM((1, 3, 4, 104, 128), F32),
            pltpu.VMEM((4, 3, 1, 104, 128), F32),
            pltpu.VMEM((1, 7, 104, 128), F32),
            pltpu.VMEM((3, 2, 4, 104, 128), F32),
            pltpu.VMEM((12, 2, 256), F32),
            pltpu.VMEM((12, 2, 256), F32),
            pltpu.VMEM((8, Q + 8), F32),
            pltpu.VMEM((24, B), F32),
            pltpu.VMEM((4, 1, 4, 128), F32),
            pltpu.VMEM((4, 3, 4, 128), F32),
            pltpu.VMEM((2, 4, 2, 128), F32),
            pltpu.VMEM((2, 1, 4, 2, 128), F32),
            pltpu.VMEM((2, 4, 1, 2, 128), F32),
            pltpu.VMEM((4, 1, 4, 128), F32),
            pltpu.VMEM((4, 4, 128), F32),
            dma((8,)),
            dma((2,)),
            dma((2,)),
            dma((3, 4)),
            dma((1, 3, 4)),
            dma((3, 4)),
            dma((3, 4)),
            dma((2,)),
            dma((2,)),
            dma((2, 4)),
            dma((2, 1, 4)),
            dma((2, 4)),
            dma((2, 4)),
            dma((3, 4)),
            dma((3, 4)),
            dma((4,)),
            dma((4,)),
        ],
        compiler_params=pltpu.CompilerParams(
            collective_id=0, has_side_effects=True, vmem_limit_bytes=60 << 20
        ),
    )(
        neighbours,
        residual.reshape(8, B),
        previous.reshape(8, B),
        jnp.transpose(restrict, (1, 0, 2)).reshape(Q, B),
        factor(lower),
        factor(pivot),
        factor(upper),
        jnp.transpose(couple, (0, 1, 4, 2, 3)).reshape(4, 2, Q, B),
    )
    return result.reshape(4, 2, B)


def solution(mesh):
    placed = (
        P("patch", "line", None),
        P("patch", "line", None),
        P("patch", "line", None, None),
        P("patch", "line", None, None),
        P("patch", "line", None, None),
        P("patch", "line", None, None, None),
        P(),
        P("patch", None),
    )
    return jax.shard_map(
        per_device, mesh=mesh, in_specs=placed, out_specs=P("patch", "line", None), check_vma=False
    )
```
